256 devices in a mesh: tens: 64 (over z, y, core), mat: 4 (over x).
Axes of the slice: x: 4, y: 4, z: 8, core: 2. Of those that a mesh axis runs over, the one named last changes fastest.
Arguments:
- tiles: bfloat16 [2048, 64, 4096], P(('tens', 'mat')), may hold values from -6 to 6
- tile_dest: int32 [2048], P(('tens', 'mat')), may hold values from 0 to 63
- tile_aux: int32 [2048], P(('tens', 'mat')), may hold values from 0 to 1
- tile_row: int32 [2048], P(('tens', 'mat')), may hold values from 0 to 15
- tile_col: int32 [2048], P(('tens', 'mat')), may hold values from 0 to 15
- green_occ: bfloat16 [1024, 1024], P(('tens', 'mat')), may hold values from -0.75 to 0.75
- green_virt: bfloat16 [1024, 1024], P(('tens', 'mat')), may hold values from -0.75 to 0.75
Outputs:
- chi: float32 [8192, 64], P('tens')
The draws below stay inside these ranges and needn't reach their ends.
All inputs are finite; a program needn't handle non-finite values.
Results may differ from the reference program's by a relative error of at most 0.0041.
Values may be sent and summed in bfloat16 or wider, within the bound.
No kernel may reach another device: no remote copies, remote signals or barrier semaphores. Data moves between devices by JAX's collectives and lax.ppermute only.
A program may use at most 128 MiB of HBM per device.

```python
import jax
import jax.numpy as jnp
from jax import lax

BS = 64
NA = 16
AUXB_DEV = 2
NP = 128
TILES = 2048
N_TENS = 64


def set_ends(entries, stream_key, smallest, high):
    extent = entries.shape
    spot = [jax.random.randint(jax.random.fold_in(stream_key, axis), (), 0, extent[axis]) for axis in range(len(extent))]
    entries = entries.at[tuple(spot)].set(smallest)
    longest = extent.index(max(extent))
    spot[longest] = (spot[longest] + 1) % extent[longest]
    return entries.at[tuple(spot)].set(high)


def shard_levels(own_key, shape, pieces, least, largest):
    gain, own = 1.0, jax.random.fold_in(own_key, 6)
    for dim, shards_of in pieces:
        draws = jnp.exp(jax.random.uniform(jax.random.fold_in(own, dim), (shards_of,), jnp.float32, least / len(pieces), largest / len(pieces)))
        gain = gain * jnp.repeat(draws, shape[dim] // shards_of).reshape([-1 if axis == dim else 1 for axis in range(len(shape))])
    return gain


def scatter_about(rng, shape, deviation, reach, split=(), kind=jnp.bfloat16):
    values = jax.random.normal(rng, shape, jnp.float32) * deviation
    if len(split) > 0:
        values = shard_levels(rng, shape, split, -0.22, 0.18) * values
    return jnp.clip(values, min=-reach, max=reach).astype(kind)


def setup_inputs(seed: int = 0) -> dict:
    splits = jax.random.split(jax.random.key(seed), 8)
    tiles = scatter_about(splits[0], (TILES, BS, BS * BS), 1.0, 6.0, ((0, 256),))
    tile_dest = set_ends(jax.random.randint(splits[1], (TILES,), 0, N_TENS), jax.random.fold_in(splits[1], 1), 0, N_TENS - 1).astype(jnp.int32)
    tile_aux = set_ends(jax.random.randint(splits[2], (TILES,), 0, AUXB_DEV), jax.random.fold_in(splits[2], 1), 0, AUXB_DEV - 1).astype(jnp.int32)
    tile_row = set_ends(jax.random.randint(splits[3], (TILES,), 0, NA), jax.random.fold_in(splits[3], 1), 0, NA - 1).astype(jnp.int32)
    tile_col = set_ends(jax.random.randint(splits[4], (TILES,), 0, NA), jax.random.fold_in(splits[4], 1), 0, NA - 1).astype(jnp.int32)
    green_occ = scatter_about(splits[5], (NA * BS, NA * BS), BS ** -0.5, 0.75, ((0, 256),))
    green_virt = scatter_about(splits[6], (NA * BS, NA * BS), BS ** -0.5, 0.75, ((0, 256),))
    return dict(tiles=tiles, tile_dest=tile_dest, tile_aux=tile_aux, tile_row=tile_row, tile_col=tile_col, green_occ=green_occ, green_virt=green_virt)


def pick_block(grid, row, col):
    zero = jnp.zeros((), jnp.int32)
    piece = lax.dynamic_slice(grid, (row, zero, col, zero), (1, BS, 1, BS))
    return piece.reshape(BS, BS).astype(jnp.float32)


def settle(value):
    return lax.optimization_barrier(value.astype(jnp.bfloat16)).astype(jnp.float32)


def reference(tiles, tile_dest, tile_aux, tile_row, tile_col, green_occ, green_virt):
    blocks = tiles.reshape(TILES, BS, BS, BS)
    occ_grid = green_occ.reshape(NA, BS, NA, BS)
    virt_grid = green_virt.reshape(NA, BS, NA, BS)
    high = lax.Precision.HIGHEST

    def add_tile(carry, index):
        block = lax.dynamic_index_in_dim(blocks, index, 0, keepdims=False).astype(jnp.float32)
        row = lax.dynamic_index_in_dim(tile_row, index, 0, keepdims=False).astype(jnp.int32)
        col = lax.dynamic_index_in_dim(tile_col, index, 0, keepdims=False).astype(jnp.int32)
        virt_cc = pick_block(virt_grid, col, col)
        virt_cr = pick_block(virt_grid, col, row)
        occ_rr = pick_block(occ_grid, row, row)
        occ_rc = pick_block(occ_grid, row, col)
        upper = settle(jnp.einsum("pmn,nj->pmj", block, virt_cc, precision=high))
        wider = settle(jnp.einsum("pmn,ni->pmi", block, virt_cr, precision=high))
        yonder = settle(jnp.einsum("mi,qij->qmj", occ_rr, block, precision=high))
        crossing = settle(jnp.einsum("mj,qij->qmi", occ_rc, block, precision=high))
        direct = jnp.einsum("pmj,qmj->pq", upper, yonder, precision=high)
        swapped = jnp.einsum("pmi,qmi->pq", wider, crossing, precision=high)
        pair = (direct + swapped) / BS
        owner = lax.dynamic_index_in_dim(tile_dest, index, 0, keepdims=False).astype(jnp.int32)
        local = lax.dynamic_index_in_dim(tile_aux, index, 0, keepdims=False).astype(jnp.int32)
        target = owner * AUXB_DEV + local
        current = lax.dynamic_index_in_dim(carry, target, 0, keepdims=False)
        carry = lax.dynamic_update_index_in_dim(carry, current + pair, target, 0)
        return carry, None

    start = jnp.zeros((NP, BS, BS), jnp.float32)
    result, unused = lax.scan(add_tile, start, jnp.arange(TILES, dtype=jnp.int32))
    return result.reshape(NP * BS, BS)
```

```python
import jax
import jax.numpy as jnp
from jax import lax
from jax.sharding import Mesh, PartitionSpec as P

BS = 64
NA = 16
AUX = 2
ZH = ("z", "h")
ZHL = ("z", "h", "l")
TENS = ("z", "h", "l", "c")
ALL = ("z", "h", "l", "c", "x")
NX = 4


def shift(values, k):
    return lax.ppermute(values, "x", [(i, (i + k) % NX) for i in range(NX)])


def by_x(parts, me):
    stacked = jnp.stack(parts)
    return jnp.take(stacked, (me - jnp.arange(NX)) % NX, axis=0)


def shards(tiles, tile_dest, tile_aux, tile_row, tile_col, green_occ, green_virt):
    count = tiles.shape[0]
    me = lax.axis_index("x")
    info = jnp.stack([tile_row, tile_col, tile_dest * AUX + tile_aux])
    infos = [info] + [shift(info, k) for k in range(1, NX)]

    with jax.named_scope("gather_rows"):
        own = jnp.stack([green_occ, green_virt]).reshape(2, 4, NA, BS)
        own = own.transpose(0, 2, 1, 3).reshape(2 * NA, 4 * BS)
        rows = lax.all_to_all(jnp.broadcast_to(own[None], (32, 2 * NA, 4 * BS)), ZHL, 0, 0)
        other = lax.ppermute(rows, "c", [(0, 1), (1, 0)])
        core = lax.axis_index("c")
        both = jnp.where(core == 0, jnp.stack([rows, other]), jnp.stack([other, rows]))
        table = both.reshape(2, NA, 2, 2, NA, 4 * BS)

    with jax.named_scope("pick_blocks"):
        def pick(which, row, col):
            ids = jnp.arange(NA * NA, dtype=jnp.int32)
            hot = ((row * NA + col)[..., None] == ids).astype(jnp.bfloat16)
            hot = hot.reshape(row.shape + (NA, NA))
            return jnp.einsum("tbk,cblkv->tlcv", hot, table[:, :, :, which],
                              preferred_element_type=jnp.float32).astype(jnp.bfloat16)

        def for_device(info):
            r, c = info[0], info[1]
            return jnp.stack([pick(1, c, c), pick(1, c, r), pick(0, r, r), pick(0, r, c)])

        mine = for_device(infos[0])
        got = [mine] + [None] * (NX - 1)
        for k in range(1, NX):
            got[NX - k] = shift(for_device(infos[k]), NX - k)
        blocks = by_x(got, me)
        blocks = blocks.reshape(NX, 4, count, 2, 2, 4, BS).transpose(1, 2, 3, 4, 0, 5, 6)
        blocks = blocks.reshape(4, count, BS, BS)

    with jax.named_scope("products"):
        cube = tiles.reshape(count, BS, BS, BS)
        f32 = jnp.float32
        upper = jnp.einsum("bpmn,bnj->bpmj", cube, blocks[0], preferred_element_type=f32).astype(jnp.bfloat16)
        wider = jnp.einsum("bpmn,bni->bpmi", cube, blocks[1], preferred_element_type=f32).astype(jnp.bfloat16)
        yonder = jnp.einsum("bmi,bqij->bqmj", blocks[2], cube, preferred_element_type=f32).astype(jnp.bfloat16)
        crossing = jnp.einsum("bmj,bqij->bqmi", blocks[3], cube, preferred_element_type=f32).astype(jnp.bfloat16)
        pair = jnp.einsum("bpmj,bqmj->bpq", upper, yonder, preferred_element_type=f32)
        pair = pair + jnp.einsum("bpmi,bqmi->bpq", wider, crossing, preferred_element_type=f32)
        pair = pair * (1.0 / BS)

    with jax.named_scope("owners"):
        part = BS * BS // NX
        split = pair.astype(jnp.bfloat16).reshape(count, NX, part)
        terms = [lax.dynamic_index_in_dim(split, me, 1, keepdims=False)]
        for k in range(1, NX):
            terms.append(shift(lax.dynamic_index_in_dim(split, (me + k) % NX, 1, keepdims=False), k))
        terms = jnp.concatenate(terms)
        target = jnp.concatenate([i[2] for i in infos])
        hot = (jnp.arange(128, dtype=jnp.int32)[:, None] == target[None, :]).astype(jnp.bfloat16)
        dense = jnp.dot(hot, terms, preferred_element_type=jnp.float32).astype(jnp.bfloat16)
        spread = lax.all_to_all(dense.reshape(64, 16, 128), TENS, 0, 0)
        owned = jnp.sum(spread.astype(jnp.float32), axis=0).reshape(AUX, part)
        owned = by_x([owned] + [shift(owned, k) for k in range(1, NX)], me)
        return owned.transpose(1, 0, 2).reshape(AUX * BS, BS)


def solution(mesh):
    fine = Mesh(mesh.devices.reshape(8, 2, 2, 2, 4), ALL)
    return jax.shard_map(
        shards,
        mesh=fine,
        in_specs=(P(ALL, None, None), P(ALL), P(ALL), P(ALL), P(ALL), P(ALL, None), P(ALL, None)),
        out_specs=P(TENS, None),
        check_vma=False,
    )
```

```python
import jax
import jax.numpy as jnp
from jax import lax
from jax.experimental import pallas as pl
from jax.experimental.pallas import tpu as pltpu
from jax.sharding import Mesh, PartitionSpec as P

BS = 64
NA = 16
AUX = 2
ZHL = ("z", "h", "l")
TENS = ("z", "h", "l", "c")
ALL = ("z", "h", "l", "c", "x")
NX = 4
F32, BF16 = jnp.float32, jnp.bfloat16
VMEM = pl.BlockSpec(memory_space=pltpu.VMEM)
SMEM = pl.BlockSpec(memory_space=pltpu.SMEM)


def shift(values, k):
    return lax.ppermute(values, "x", [(i, (i + k) % NX) for i in range(NX)])


def nt(a, b):
    return lax.dot_general(a, b, (((1,), (1,)), ((), ())), preferred_element_type=F32)


def eye(n):
    rows = lax.broadcasted_iota(jnp.int32, (n, n), 0)
    return jnp.where(rows == lax.broadcasted_iota(jnp.int32, (n, n), 1), 1.0, 0.0).astype(BF16)


def swap_kernel(t_ref, o_ref, scr):
    wide, narrow = eye(256), eye(128)
    for s in range(16):
        cut = slice(s * 256, s * 256 + 256)
        scr[cut, :] = nt(wide, jnp.concatenate([t_ref[0, :, cut], t_ref[1, :, cut]], axis=0))
    for s in range(16):
        cut = slice(s * 256, s * 256 + 256)
        rows = jnp.concatenate([scr[pl.ds(4 * s + k, BS, stride=BS), :] for k in range(4)], axis=0)
        back = nt(narrow, rows.astype(BF16)).astype(BF16)
        o_ref[0, :, cut] = back[:BS]
        o_ref[1, :, cut] = back[BS:]


def swap(tiles):
    count = tiles.shape[0]
    spec = pl.BlockSpec((2, BS, BS * BS), lambda i: (i, 0, 0))
    return pl.pallas_call(
        swap_kernel,
        grid=(count // 2,),
        out_shape=jax.ShapeDtypeStruct(tiles.shape, tiles.dtype),
        in_specs=[spec],
        out_specs=spec,
        scratch_shapes=[pltpu.VMEM((BS * BS, 128), F32)],
        cost_estimate=pl.CostEstimate(flops=3_000_000_000, bytes_accessed=2 * tiles.size * 2, transcendentals=0),
        compiler_params=pltpu.CompilerParams(vmem_limit_bytes=32 * 1024 * 1024),
        name="swap",
    )(tiles)


def pick_kernel(core_ref, hot_ref, own_ref, other_ref, o_ref):
    core = core_ref[0]
    for side, ref in ((core, own_ref), (1 - core, other_ref)):
        for l in range(2):
            for ih in range(2):
                for arr in range(2):
                    first = (ih * 2 + arr) * NA
                    table = jnp.concatenate([ref[2 * b + l, first:first + NA, :] for b in range(NA)], axis=0)
                    got = jnp.dot(hot_ref[arr], table, preferred_element_type=F32).astype(BF16)
                    for k in range(NX):
                        o_ref[k, l, side, ih, arr] = got[k * NA:(k + 1) * NA]


def tile_kernel(me_ref, t_ref, ts_ref, g0, g1, g2, g3, o_ref, gscr, scr, yz):
    step = pl.program_id(0)
    me = me_ref[0]

    @pl.when(step == 0)
    def _():
        for k, ref in enumerate((g0, g1, g2, g3)):
            start = pl.multiple_of(((me - k + NX) & 3) * 256, 256)
            gscr[pl.ds(start, 256), :] = ref[...].reshape(256, 128).astype(F32)

    m = lax.broadcasted_iota(jnp.int32, (BS, BS), 0)
    place = ((m & 1) << 5) + (((m >> 2) & 3) << 3) + ((m >> 5) << 2) + (((m >> 4) & 1) << 1) + ((m >> 1) & 1)
    order = jnp.where(place == lax.broadcasted_iota(jnp.int32, (BS, BS), 1), 1.0, 0.0).astype(BF16)
    low = lax.broadcasted_iota(jnp.int32, (32, 128), 1) < BS
    low64 = lax.broadcasted_iota(jnp.int32, (BS, 128), 1) < BS

    def halves(arr, q):
        rows = gscr[pl.ds(arr * 16 + step * 2 + q, 32, stride=32), :]
        turned = pltpu.roll(rows, BS, 1)
        both = jnp.concatenate([jnp.where(low, rows, turned), jnp.where(low, turned, rows)], axis=0)
        block = jnp.dot(order, both.astype(BF16), preferred_element_type=F32)
        return jnp.where(low64, block, 0.0), jnp.where(low64, 0.0, block)

    def twice_t(q):
        return jnp.concatenate(halves(1, q), axis=0).T.astype(BF16)

    def four(q):
        left, right = (h.astype(BF16) for h in halves(0, q))
        none = jnp.zeros((BS, 128), BF16)
        return jnp.concatenate([
            jnp.concatenate([jnp.concatenate([left, none], axis=1), jnp.concatenate([right, none], axis=1)], axis=0),
            jnp.concatenate([jnp.concatenate([none, left], axis=1), jnp.concatenate([none, right], axis=1)], axis=0),
        ], axis=0)

    virt = jnp.concatenate([twice_t(0), twice_t(1)], axis=1)
    zero = jnp.zeros((BS, 128), BF16)
    for s in range(16):
        a = t_ref[0, :, s * 256:s * 256 + 128]
        b = t_ref[0, :, s * 256 + 128:s * 256 + 256]
        left = jnp.concatenate([a, zero, b, zero], axis=0)
        right = jnp.concatenate([zero, a, zero, b], axis=0)
        out = nt(virt, jnp.concatenate([left, right], axis=1))
        scr[s * 256:s * 256 + 128, :] = out[:, :128]
        scr[s * 256 + 128:s * 256 + 256, :] = out[:, 128:]
    same, cross = four(0), four(1)
    for s in range(16):
        cut = slice(s * 256, s * 256 + 256)
        yz[:BS, cut] = nt(ts_ref[0, :, cut], same).astype(BF16)
    for s in range(16):
        cut = slice(s * 256, s * 256 + 256)
        yz[BS:, cut] = nt(t_ref[0, :, cut], cross).astype(BF16)
    acc = jnp.zeros((128, 128), F32)
    for s in range(16):
        rows = jnp.concatenate([scr[pl.ds(4 * s + k, BS, stride=BS), :] for k in range(4)], axis=0)
        acc += jnp.dot(yz[:, s * 256:s * 256 + 256], rows.astype(BF16), preferred_element_type=F32)
    turned = acc.T * (1.0 / BS)
    pair = turned[:BS] + pltpu.roll(turned[BS:], BS, 1)
    packed = jnp.where(low, pair[:32], pltpu.roll(pair[32:], BS, 1))
    for k in range(NX):
        o_ref[k, 0] = packed[8 * k:8 * k + 8]


def tile_pairs(me, tiles, swapped, got):
    count = tiles.shape[0]
    tile = pl.BlockSpec((1, BS, BS * BS), lambda i: (i, 0, 0))
    return pl.pallas_call(
        tile_kernel,
        grid=(count,),
        out_shape=jax.ShapeDtypeStruct((NX, count, 8, 128), F32),
        in_specs=[SMEM, tile, tile] + [VMEM] * 4,
        out_specs=pl.BlockSpec((NX, 1, 8, 128), lambda i: (0, i, 0, 0)),
        scratch_shapes=[pltpu.VMEM((1024, 128), F32), pltpu.VMEM((BS * BS, 128), F32), pltpu.VMEM((128, BS * BS), BF16)],
        compiler_params=pltpu.CompilerParams(vmem_limit_bytes=32 * 1024 * 1024),
        name="tile_pairs",
    )(me, tiles, swapped, *got)


def place_kernel(i0, i1, i2, i3, t0, t1, t2, t3, o_ref, total):
    total[...] = jnp.zeros_like(total)
    for info, terms in ((i0, t0), (i1, t1), (i2, t2), (i3, t3)):
        for t in range(terms.shape[0]):
            at = info[2, t]
            total[at] += terms[t]
    o_ref[...] = total[...].reshape(o_ref.shape).astype(BF16)


def place(infos, terms):
    return pl.pallas_call(
        place_kernel,
        out_shape=jax.ShapeDtypeStruct((64, 16, 128), BF16),
        in_specs=[SMEM] * 4 + [VMEM] * 4,
        out_specs=VMEM,
        scratch_shapes=[pltpu.VMEM((128, 8, 128), F32)],
        name="place",
    )(*infos, *terms)


def sum_kernel(s_ref, o_ref):
    o_ref[...] = jnp.sum(s_ref[...].astype(F32), axis=0)


def finish_kernel(me_ref, p0, p1, p2, p3, o_ref, whole):
    me = me_ref[0]
    for k, ref in enumerate((p0, p1, p2, p3)):
        x = (me - k + NX) & 3
        for aux in range(AUX):
            whole[aux, x] = ref[8 * aux:8 * aux + 8]
    for aux in range(AUX):
        rows = whole[aux].reshape(32, 128)
        o_ref[aux * BS:aux * BS + 32, :] = rows[:, :BS]
        o_ref[aux * BS + 32:(aux + 1) * BS, :] = pltpu.roll(rows, BS, 1)[:, :BS]


def shards(tiles, tile_dest, tile_aux, tile_row, tile_col, green_occ, green_virt):
    count = tiles.shape[0]
    x = lax.axis_index("x")
    me = x.reshape(1)
    info = jnp.stack([tile_row, tile_col, tile_dest * AUX + tile_aux])
    infos = [info] + [shift(info, k) for k in range(1, NX)]

    with jax.named_scope("gather_rows"):
        own = jnp.stack([green_occ, green_virt]).reshape(2, 2, 2, NA, BS)
        own = own.transpose(1, 0, 3, 2, 4).reshape(4 * NA, 2 * BS)
        rows = lax.all_to_all(jnp.broadcast_to(own[None], (32, 4 * NA, 2 * BS)), ZHL, 0, 0)
        other = lax.ppermute(rows, "c", [(0, 1), (1, 0)])
    swapped = swap(tiles)

    with jax.named_scope("pick_blocks"):
        r, c = (jnp.stack([i[j] for i in infos]) for j in (0, 1))
        occ = jnp.stack([r * NA + r, r * NA + c], axis=-1)
        virt = jnp.stack([c * NA + c, c * NA + r], axis=-1)
        wanted = jnp.stack([occ, virt]).reshape(2, NX * count * 2)
        hot = (wanted[..., None] == jnp.arange(NA * NA, dtype=jnp.int32)).astype(BF16)
        picked = pl.pallas_call(
            pick_kernel,
            out_shape=jax.ShapeDtypeStruct((NX, 2, 2, 2, 2, NA, 128), BF16),
            in_specs=[SMEM] + [VMEM] * 3,
            out_specs=VMEM,
            name="pick",
        )(lax.axis_index("c").reshape(1), hot, rows, other)
        got = [picked[0]] + [None] * (NX - 1)
        for k in range(1, NX):
            got[NX - k] = shift(picked[k], NX - k)

    pairs = tile_pairs(me, tiles, swapped, got)

    with jax.named_scope("owners"):
        terms = [lax.dynamic_index_in_dim(pairs, x, 0, keepdims=False)]
        for k in range(1, NX):
            terms.append(shift(lax.dynamic_index_in_dim(pairs, (x + k) % NX, 0, keepdims=False), k))
        spread = lax.all_to_all(place(infos, terms), TENS, 0, 0)
        owned = pl.pallas_call(
            sum_kernel, out_shape=jax.ShapeDtypeStruct((16, 128), F32), in_specs=[VMEM], out_specs=VMEM, name="sum",
        )(spread)
        parts = [owned] + [shift(owned, k) for k in range(1, NX)]
        return pl.pallas_call(
            finish_kernel,
            out_shape=jax.ShapeDtypeStruct((AUX * BS, BS), F32),
            in_specs=[SMEM] + [VMEM] * 4,
            out_specs=VMEM,
            scratch_shapes=[pltpu.VMEM((AUX, NX, 8, 128), F32)],
            name="finish",
        )(me, *parts)


def solution(mesh):
    fine = Mesh(mesh.devices.reshape(8, 2, 2, 2, 4), ALL)
    return jax.shard_map(
        shards,
        mesh=fine,
        in_specs=(P(ALL, None, None), P(ALL), P(ALL), P(ALL), P(ALL), P(ALL, None), P(ALL, None)),
        out_specs=P(TENS, None),
        check_vma=False,
    )
```

```python
import jax
import jax.numpy as jnp
from jax import lax
from jax.experimental import pallas as pl
from jax.experimental.pallas import tpu as pltpu
from jax.sharding import Mesh, PartitionSpec as P

BS = 64
NA = 16
AUX = 2
ZHL = ("z", "h", "l")
TENS = ("z", "h", "l", "c")
ALL = ("z", "h", "l", "c", "x")
NX = 4
F32, BF16 = jnp.float32, jnp.bfloat16
VMEM = pl.BlockSpec(memory_space=pltpu.VMEM)
SMEM = pl.BlockSpec(memory_space=pltpu.SMEM)
LARGE, SMALL = 58 * 1024 * 1024, 12 * 1024 * 1024


def shift(values, k):
    return lax.ppermute(values, "x", [(i, (i + k) % NX) for i in range(NX)])


def nt(a, b):
    return lax.dot_general(a, b, (((1,), (1,)), ((), ())), preferred_element_type=F32)


def eye(n):
    rows = lax.broadcasted_iota(jnp.int32, (n, n), 0)
    return jnp.where(rows == lax.broadcasted_iota(jnp.int32, (n, n), 1), 1.0, 0.0).astype(BF16)


def low_lanes(rows):
    return lax.broadcasted_iota(jnp.int32, (rows, 128), 1) < BS


def rows_kernel(occ_ref, virt_ref, o_ref, scr):
    for arr, ref in enumerate((occ_ref, virt_ref)):
        values = ref[...].astype(F32)
        for i in range(4):
            for pair in range(8):
                at = (arr * 4 + i) * 8 + pair
                scr[at:at + 1, :] = values[i:i + 1, pair * 128:pair * 128 + 128]
    block = scr[...].astype(BF16)
    for peer in range(o_ref.shape[0]):
        o_ref[peer] = block


def prep_kernel(i0, i1, i2, i3, t_ref, sw_ref, tr_ref, hot_ref, scr):
    @pl.when(pl.program_id(0) == 0)
    def _():
        at = lax.broadcasted_iota(jnp.int32, (32, 256), 0)
        row = jnp.zeros((32, 256), jnp.int32)
        col = jnp.zeros((32, 256), jnp.int32)
        for k, info in enumerate((i0, i1, i2, i3)):
            for t in range(8):
                here = at == k * 8 + t
                row = jnp.where(here, info[0, t], row)
                col = jnp.where(here, info[1, t], col)
        lane = lax.broadcasted_iota(jnp.int32, (32, 256), 1)
        for arr, first in enumerate((row, col)):
            for q in range(2):
                second = first if q == 0 else (col if arr == 0 else row)
                for odd in range(2):
                    for i in range(2):
                        hit = (first == (lane >> 4)) & ((lane & 15) == i * 8 + (second >> 1)) & ((second & 1) == odd)
                        start = ((q * 2 + odd) * 2 + i) * 32
                        hot_ref[arr, start:start + 32, :] = jnp.where(hit, 1.0, 0.0).astype(BF16)

    wide, narrow = eye(256), eye(128)
    for s in range(16):
        cut = slice(s * 256, s * 256 + 256)
        turned = jnp.concatenate([t_ref[0, :, cut], t_ref[1, :, cut]], axis=0).T
        scr[cut, :] = turned.astype(F32)
        tr_ref[0, cut, :] = turned.astype(BF16)
    for s in range(16):
        cut = slice(s * 256, s * 256 + 256)
        rows = jnp.concatenate([scr[pl.ds(4 * s + k, BS, stride=BS), :] for k in range(4)], axis=0)
        back = rows.astype(BF16).T
        sw_ref[0, :, cut] = back[:BS]
        sw_ref[1, :, cut] = back[BS:]


def prep(infos, tiles):
    count = tiles.shape[0]
    spec = pl.BlockSpec((2, BS, BS * BS), lambda i: (i, 0, 0))
    return pl.pallas_call(
        prep_kernel,
        grid=(count // 2,),
        out_shape=(
            jax.ShapeDtypeStruct(tiles.shape, BF16),
            jax.ShapeDtypeStruct((count // 2, BS * BS, 128), BF16),
            jax.ShapeDtypeStruct((2, 256, 256), BF16),
        ),
        in_specs=[SMEM] * 4 + [spec],
        out_specs=(spec, pl.BlockSpec((1, BS * BS, 128), lambda i: (i, 0, 0)), pl.BlockSpec((2, 256, 256), lambda i: (0, 0, 0))),
        scratch_shapes=[pltpu.VMEM((BS * BS, 128), F32)],
        cost_estimate=pl.CostEstimate(flops=9_000_000_000, bytes_accessed=6 * tiles.size, transcendentals=0),
        compiler_params=pltpu.CompilerParams(vmem_limit_bytes=LARGE),
        name="prep",
    )(*infos, tiles)


def pick_kernel(core_ref, hot_ref, own_ref, other_ref, o0, o1, o2, o3):
    core = core_ref[0]
    low = low_lanes(BS)
    for side, ref in ((core, own_ref), (1 - core, other_ref)):
        for l in range(2):
            for ih in range(2):
                found = []
                for arr in range(2):
                    first = (arr * 2 + ih) * 16
                    table = jnp.concatenate([ref[2 * b + l, first:first + 16, :] for b in range(NA)], axis=0)
                    got = jnp.dot(hot_ref[arr], table, preferred_element_type=F32)
                    left = got[:BS] + pltpu.roll(got[BS:2 * BS], BS, 1)
                    right = pltpu.roll(got[2 * BS:3 * BS], BS, 1) + got[3 * BS:]
                    found.append(jnp.where(low, left, right))
                for il in range(2):
                    for k, o_ref in enumerate((o0, o1, o2, o3)):
                        start = il * 32 + k * 8
                        o_ref[l, side, ih * 2 + il] = jnp.concatenate([f[start:start + 8] for f in found], axis=0).astype(BF16)


def tile_kernel(me_ref, t_ref, sw_ref, tr_ref, g0, g1, g2, g3, o0, o1, o2, o3, gscr, us, ws, ys, zs, pk):
    step = pl.program_id(0)
    me = me_ref[0]

    @pl.when(step == 0)
    def _():
        for k, ref in enumerate((g0, g1, g2, g3)):
            start = pl.multiple_of(((me - k + NX) & 3) * 256, 256)
            gscr[pl.ds(start, 256), :] = ref[...].reshape(256, 128).astype(F32)

    m = lax.broadcasted_iota(jnp.int32, (BS, BS), 0)
    place = (((m >> 2) & 3) << 4) + ((m >> 5) << 3) + (((m >> 4) & 1) << 2) + (m & 3)
    order = jnp.where(place == lax.broadcasted_iota(jnp.int32, (BS, BS), 1), 1.0, 0.0).astype(BF16)
    low = low_lanes(BS)

    def blocks_t(arr, u):
        rows = gscr[pl.ds(arr * 8 + step * 2 + u, BS, stride=16), :].astype(BF16)
        rows = jnp.dot(order, rows, preferred_element_type=F32)
        turned = jnp.concatenate([rows, rows], axis=0).T
        return turned[:BS], turned[BS:]

    def two(b):
        return jnp.concatenate([jnp.where(low, b, 0.0), jnp.where(low, 0.0, b)], axis=0).astype(BF16)

    def four(b):
        pair = two(b)
        none = jnp.zeros((128, 128), BF16)
        return jnp.concatenate([jnp.concatenate([pair, none], axis=1), jnp.concatenate([none, pair], axis=1)], axis=0)

    (cc0, cr0), (cc1, cr1) = blocks_t(1, 0), blocks_t(1, 1)
    virt = jnp.concatenate([
        jnp.concatenate([two(cc0), two(cc1)], axis=1),
        jnp.concatenate([two(cr0), two(cr1)], axis=1),
    ], axis=0)
    low128 = low_lanes(128)
    zero = jnp.zeros((128, 128), BF16)
    for s in range(16):
        a = tr_ref[0, s * 256:s * 256 + 128, :]
        b = tr_ref[0, s * 256 + 128:s * 256 + 256, :]
        rhs = jnp.concatenate([
            jnp.concatenate([jnp.where(low128, a, zero), jnp.where(low128, b, zero)], axis=1),
            jnp.concatenate([jnp.where(low128, zero, a), jnp.where(low128, zero, b)], axis=1),
        ], axis=0)
        out = jnp.dot(virt, rhs, preferred_element_type=F32)
        for ref, first in ((us, 0), (ws, 128)):
            ref[s * 256:s * 256 + 128, :] = out[first:first + 128, :128]
            ref[s * 256 + 128:s * 256 + 256, :] = out[first:first + 128, 128:]
    for u in range(2):
        same, cross = blocks_t(0, u)
        for ref, dest, block in ((sw_ref, ys, same), (t_ref, zs, cross)):
            rows = jnp.concatenate([ref[u, :, s * 256:s * 256 + 256] for s in range(16)], axis=0)
            out = jnp.dot(rows, four(block), preferred_element_type=F32).astype(BF16)
            for s in range(16):
                dest[u * BS:u * BS + BS, s * 256:s * 256 + 256] = out[s * BS:s * BS + BS]
    acc = jnp.zeros((128, 128), F32)
    for left, right in ((ys, us), (zs, ws)):
        for s in range(16):
            rows = jnp.concatenate([right[pl.ds(4 * s + k, BS, stride=BS), :] for k in range(4)], axis=0)
            acc += jnp.dot(left[:, s * 256:s * 256 + 256], rows.astype(BF16), preferred_element_type=F32)
    acc = acc.T * (1.0 / BS)
    low32 = low_lanes(32)
    pk[0] = jnp.where(low32, acc[:32], pltpu.roll(acc[32:64], BS, 1))
    pk[1] = jnp.where(low32, pltpu.roll(acc[64:96], BS, 1), acc[96:])
    for k, o_ref in enumerate((o0, o1, o2, o3)):
        start = pl.multiple_of(((me + k) & 3) * 8, 8)
        for u in range(2):
            o_ref[u] = pk[u, pl.ds(start, 8), :]


def tile_pairs(me, tiles, swapped, turned, got):
    count = tiles.shape[0]
    tile = pl.BlockSpec((2, BS, BS * BS), lambda i: (i, 0, 0))
    return pl.pallas_call(
        tile_kernel,
        grid=(count // 2,),
        out_shape=[jax.ShapeDtypeStruct((count, 8, 128), F32)] * NX,
        in_specs=[SMEM, tile, tile, pl.BlockSpec((1, BS * BS, 128), lambda i: (i, 0, 0))] + [VMEM] * 4,
        out_specs=[pl.BlockSpec((2, 8, 128), lambda i: (i, 0, 0))] * NX,
        scratch_shapes=[
            pltpu.VMEM((1024, 128), F32), pltpu.VMEM((BS * BS, 128), F32), pltpu.VMEM((BS * BS, 128), F32),
            pltpu.VMEM((128, BS * BS), BF16), pltpu.VMEM((128, BS * BS), BF16), pltpu.VMEM((2, 32, 128), F32),
        ],
        compiler_params=pltpu.CompilerParams(vmem_limit_bytes=LARGE),
        name="tile_pairs",
    )(me, tiles, swapped, turned, *got)


def place_kernel(i0, i1, i2, i3, t0, t1, t2, t3, o_ref, total):
    total[...] = jnp.zeros_like(total)
    for info, terms in ((i0, t0), (i1, t1), (i2, t2), (i3, t3)):
        for t in range(terms.shape[0]):
            at = info[2, t]
            total[at] += terms[t]
    o_ref[...] = total[...].reshape(o_ref.shape).astype(BF16)


def place(infos, terms):
    return pl.pallas_call(
        place_kernel,
        out_shape=jax.ShapeDtypeStruct((64, 16, 128), BF16),
        in_specs=[SMEM] * 4 + [VMEM] * 4,
        out_specs=VMEM,
        scratch_shapes=[pltpu.VMEM((128, 8, 128), F32)],
        compiler_params=pltpu.CompilerParams(vmem_limit_bytes=SMALL),
        name="place",
    )(*infos, *terms)


def sum_kernel(s_ref, o_ref):
    o_ref[...] = jnp.sum(s_ref[...].astype(F32), axis=0)


def finish_kernel(me_ref, p0, p1, p2, p3, o_ref, whole):
    me = me_ref[0]
    for k, ref in enumerate((p0, p1, p2, p3)):
        x = (me - k + NX) & 3
        for aux in range(AUX):
            whole[aux, x] = ref[8 * aux:8 * aux + 8]
    for aux in range(AUX):
        rows = whole[aux].reshape(32, 128)
        o_ref[aux * BS:aux * BS + 32, :] = rows[:, :BS]
        o_ref[aux * BS + 32:(aux + 1) * BS, :] = pltpu.roll(rows, BS, 1)[:, :BS]


def shards(tiles, tile_dest, tile_aux, tile_row, tile_col, green_occ, green_virt):
    count = tiles.shape[0]
    x = lax.axis_index("x")
    me = x.reshape(1)
    info = jnp.stack([tile_row, tile_col, tile_dest * AUX + tile_aux])
    infos = [info] + [shift(info, k) for k in range(1, NX)]

    with jax.named_scope("gather_rows"):
        own = pl.pallas_call(
            rows_kernel,
            out_shape=jax.ShapeDtypeStruct((32, BS, 128), BF16),
            in_specs=[VMEM] * 2,
            out_specs=VMEM,
            scratch_shapes=[pltpu.VMEM((BS, 128), F32)],
            compiler_params=pltpu.CompilerParams(vmem_limit_bytes=SMALL),
            name="rows",
        )(green_occ, green_virt)
        rows = lax.all_to_all(own, ZHL, 0, 0)
        other = lax.ppermute(rows, "c", [(0, 1), (1, 0)])
    swapped, turned, hot = prep(infos, tiles)

    with jax.named_scope("pick_blocks"):
        picked = pl.pallas_call(
            pick_kernel,
            out_shape=[jax.ShapeDtypeStruct((2, 2, 4, 2 * count, 128), BF16)] * NX,
            in_specs=[SMEM] + [VMEM] * 3,
            out_specs=[VMEM] * NX,
            compiler_params=pltpu.CompilerParams(vmem_limit_bytes=SMALL),
            name="pick",
        )(lax.axis_index("c").reshape(1), hot, rows, other)
        got = [picked[0]] + [shift(picked[NX - k], k) for k in range(1, NX)]

    quarters = tile_pairs(me, tiles, swapped, turned, got)

    with jax.named_scope("owners"):
        terms = [quarters[0]] + [shift(quarters[k], k) for k in range(1, NX)]
        spread = lax.all_to_all(place(infos, terms), TENS, 0, 0)
        owned = pl.pallas_call(
            sum_kernel, out_shape=jax.ShapeDtypeStruct((16, 128), F32), in_specs=[VMEM], out_specs=VMEM,
            compiler_params=pltpu.CompilerParams(vmem_limit_bytes=SMALL), name="sum",
        )(spread)
        parts = [owned] + [shift(owned, k) for k in range(1, NX)]
        return pl.pallas_call(
            finish_kernel,
            out_shape=jax.ShapeDtypeStruct((AUX * BS, BS), F32),
            in_specs=[SMEM] + [VMEM] * 4,
            out_specs=pl.BlockSpec((AUX * BS, BS), lambda: (0, 0)),
            scratch_shapes=[pltpu.VMEM((AUX, NX, 8, 128), F32)],
            compiler_params=pltpu.CompilerParams(vmem_limit_bytes=SMALL),
            name="finish",
        )(me, *parts)


def solution(mesh):
    fine = Mesh(mesh.devices.reshape(8, 2, 2, 2, 4), ALL)
    return jax.shard_map(
        shards,
        mesh=fine,
        in_specs=(P(ALL, None, None), P(ALL), P(ALL), P(ALL), P(ALL), P(ALL, None), P(ALL, None)),
        out_specs=P(TENS, None),
        check_vma=False,
    )
```

```python
import jax
import jax.numpy as jnp
from jax import lax
from jax.experimental import pallas as pl
from jax.experimental.pallas import tpu as pltpu
from jax.sharding import Mesh, PartitionSpec as P

BS = 64
NA = 16
AUX = 2
ZHL = ("z", "h", "l")
TENS = ("z", "h", "l", "c")
ALL = ("z", "h", "l", "c", "x")
NX = 4
F32, BF16 = jnp.float32, jnp.bfloat16
VMEM = pl.BlockSpec(memory_space=pltpu.VMEM)
SMEM = pl.BlockSpec(memory_space=pltpu.SMEM)
LARGE, SMALL = 58 * 1024 * 1024, 12 * 1024 * 1024
PITCH = 65


def shift(values, k):
    return lax.ppermute(values, "x", [(i, (i + k) % NX) for i in range(NX)])


def nt(a, b):
    return lax.dot_general(a, b, (((1,), (1,)), ((), ())), preferred_element_type=F32)


def low_lanes(rows):
    return lax.broadcasted_iota(jnp.int32, (rows, 128), 1) < BS


def rows_kernel(occ_ref, virt_ref, o_ref, scr):
    for arr, ref in enumerate((occ_ref, virt_ref)):
        values = ref[...].astype(F32)
        for i in range(4):
            for pair in range(8):
                at = (arr * 4 + i) * 8 + pair
                scr[at:at + 1, :] = values[i:i + 1, pair * 128:pair * 128 + 128]
    block = scr[...].astype(BF16)
    for peer in range(o_ref.shape[0]):
        o_ref[peer] = block


def prep_kernel(i0, i1, i2, i3, t_ref, sw_ref, tr_ref, hot_ref, scr):
    @pl.when(pl.program_id(0) == 0)
    def _():
        at = lax.broadcasted_iota(jnp.int32, (32, 256), 0)
        row = jnp.zeros((32, 256), jnp.int32)
        col = jnp.zeros((32, 256), jnp.int32)
        for k, info in enumerate((i0, i1, i2, i3)):
            for t in range(8):
                here = at == k * 8 + t
                row = jnp.where(here, info[0, t], row)
                col = jnp.where(here, info[1, t], col)
        lane = lax.broadcasted_iota(jnp.int32, (32, 256), 1)
        for arr, first in enumerate((row, col)):
            for q in range(2):
                second = first if q == 0 else (col if arr == 0 else row)
                for odd in range(2):
                    for i in range(2):
                        hit = (first == (lane >> 4)) & ((lane & 15) == i * 8 + (second >> 1)) & ((second & 1) == odd)
                        start = ((q * 2 + odd) * 2 + i) * 32
                        hot_ref[arr, start:start + 32, :] = jnp.where(hit, 1.0, 0.0).astype(BF16)

    for s in range(16):
        cut = slice(s * 256, s * 256 + 256)
        turned = jnp.concatenate([t_ref[0, :, cut], t_ref[1, :, cut]], axis=0).T
        for k in range(4):
            at = (4 * s + k) * PITCH
            scr[at:at + BS, :] = turned[k * BS:k * BS + BS].astype(F32)
        tr_ref[0, cut, :] = turned.astype(BF16)
    for s in range(16):
        cut = slice(s * 256, s * 256 + 256)
        rows = jnp.concatenate([scr[pl.ds(4 * s + k, BS, stride=PITCH), :] for k in range(4)], axis=0)
        back = rows.astype(BF16).T
        sw_ref[0, :, cut] = back[:BS]
        sw_ref[1, :, cut] = back[BS:]


def prep(infos, tiles):
    count = tiles.shape[0]
    spec = pl.BlockSpec((2, BS, BS * BS), lambda i: (i, 0, 0))
    return pl.pallas_call(
        prep_kernel,
        grid=(count // 2,),
        out_shape=(
            jax.ShapeDtypeStruct(tiles.shape, BF16),
            jax.ShapeDtypeStruct((count // 2, BS * BS, 128), BF16),
            jax.ShapeDtypeStruct((2, 256, 256), BF16),
        ),
        in_specs=[SMEM] * 4 + [spec],
        out_specs=(spec, pl.BlockSpec((1, BS * BS, 128), lambda i: (i, 0, 0)), pl.BlockSpec((2, 256, 256), lambda i: (0, 0, 0))),
        scratch_shapes=[pltpu.VMEM((BS * PITCH, 128), F32)],
        cost_estimate=pl.CostEstimate(flops=9_000_000_000, bytes_accessed=6 * tiles.size, transcendentals=0),
        compiler_params=pltpu.CompilerParams(vmem_limit_bytes=LARGE),
        name="prep",
    )(*infos, tiles)


def pick_kernel(core_ref, hot_ref, own_ref, other_ref, o0, o1, o2, o3):
    core = core_ref[0]
    low = low_lanes(BS)
    for side, ref in ((core, own_ref), (1 - core, other_ref)):
        for l in range(2):
            for ih in range(2):
                found = []
                for arr in range(2):
                    first = (arr * 2 + ih) * 16
                    table = jnp.concatenate([ref[2 * b + l, first:first + 16, :] for b in range(NA)], axis=0)
                    got = jnp.dot(hot_ref[arr], table, preferred_element_type=F32)
                    left = got[:BS] + pltpu.roll(got[BS:2 * BS], BS, 1)
                    right = pltpu.roll(got[2 * BS:3 * BS], BS, 1) + got[3 * BS:]
                    found.append(jnp.where(low, left, right))
                for il in range(2):
                    for k, o_ref in enumerate((o0, o1, o2, o3)):
                        start = il * 32 + k * 8
                        o_ref[l, side, ih * 2 + il] = jnp.concatenate([f[start:start + 8] for f in found], axis=0).astype(BF16)


def tile_kernel(me_ref, t_ref, sw_ref, tr_ref, g0, g1, g2, g3, o0, o1, o2, o3, gscr, us, ws, ys, zs, pk):
    step = pl.program_id(0)
    me = me_ref[0]

    @pl.when(step == 0)
    def _():
        for k, ref in enumerate((g0, g1, g2, g3)):
            first = ((me - k + NX) & 3) * 4
            for l in range(2):
                for c in range(2):
                    for i in range(4):
                        at = pl.multiple_of((first + (l * 32 + c * 16 + i)) * 24, 8)
                        gscr[pl.ds(at, 16), :] = ref[l, c, i].astype(F32)

    low = low_lanes(BS)

    def blocks_t(arr, u):
        rows = gscr[pl.ds(arr * 8 + step * 2 + u, BS, stride=24), :]
        turned = jnp.concatenate([rows, rows], axis=0).T
        return turned[:BS], turned[BS:]

    def two(b):
        return jnp.concatenate([jnp.where(low, b, 0.0), jnp.where(low, 0.0, b)], axis=0).astype(BF16)

    def four(b):
        pair = two(b)
        none = jnp.zeros((128, 128), BF16)
        return jnp.concatenate([jnp.concatenate([pair, none], axis=1), jnp.concatenate([none, pair], axis=1)], axis=0)

    (cc0, cr0), (cc1, cr1) = blocks_t(1, 0), blocks_t(1, 1)
    virt = jnp.concatenate([
        jnp.concatenate([two(cc0), two(cc1)], axis=1),
        jnp.concatenate([two(cr0), two(cr1)], axis=1),
    ], axis=0)
    low128 = low_lanes(128)
    zero = jnp.zeros((128, 128), BF16)
    for s in range(16):
        a = tr_ref[0, s * 256:s * 256 + 128, :]
        b = tr_ref[0, s * 256 + 128:s * 256 + 256, :]
        rhs = jnp.concatenate([
            jnp.concatenate([jnp.where(low128, a, zero), jnp.where(low128, b, zero)], axis=1),
            jnp.concatenate([jnp.where(low128, zero, a), jnp.where(low128, zero, b)], axis=1),
        ], axis=0)
        out = jnp.dot(virt, rhs, preferred_element_type=F32)
        for ref, first in ((us, 0), (ws, 128)):
            for k in range(4):
                at, row, lane = (4 * s + k) * PITCH, first + (k % 2) * BS, (k // 2) * 128
                ref[at:at + BS, :] = out[row:row + BS, lane:lane + 128]
    for u in range(2):
        same, cross = blocks_t(0, u)
        for ref, dest, block in ((sw_ref, ys, same), (t_ref, zs, cross)):
            rows = jnp.concatenate([ref[u, :, s * 256:s * 256 + 256] for s in range(16)], axis=0)
            out = jnp.dot(rows, four(block), preferred_element_type=F32).astype(BF16)
            for s in range(16):
                dest[u * BS:u * BS + BS, s * 256:s * 256 + 256] = out[s * BS:s * BS + BS]
    acc = jnp.zeros((128, 128), F32)
    for left, right in ((ys, us), (zs, ws)):
        for s in range(16):
            rows = jnp.concatenate([right[pl.ds(4 * s + k, BS, stride=PITCH), :] for k in range(4)], axis=0)
            acc += jnp.dot(left[:, s * 256:s * 256 + 256], rows.astype(BF16), preferred_element_type=F32)
    acc = acc * (1.0 / BS)
    low32 = low_lanes(32)
    pk[0] = jnp.where(low32, acc[:32], pltpu.roll(acc[32:64], BS, 1))
    pk[1] = jnp.where(low32, pltpu.roll(acc[64:96], BS, 1), acc[96:])
    for k, o_ref in enumerate((o0, o1, o2, o3)):
        start = pl.multiple_of(((me + k) & 3) * 8, 8)
        for u in range(2):
            o_ref[u] = pk[u, pl.ds(start, 8), :]


def tile_pairs(me, tiles, swapped, turned, got):
    count = tiles.shape[0]
    tile = pl.BlockSpec((2, BS, BS * BS), lambda i: (i, 0, 0))
    return pl.pallas_call(
        tile_kernel,
        grid=(count // 2,),
        out_shape=[jax.ShapeDtypeStruct((count, 8, 128), F32)] * NX,
        in_specs=[SMEM, tile, tile, pl.BlockSpec((1, BS * BS, 128), lambda i: (i, 0, 0))] + [VMEM] * 4,
        out_specs=[pl.BlockSpec((2, 8, 128), lambda i: (i, 0, 0))] * NX,
        scratch_shapes=[
            pltpu.VMEM((BS * 24, 128), F32), pltpu.VMEM((BS * PITCH, 128), F32), pltpu.VMEM((BS * PITCH, 128), F32),
            pltpu.VMEM((128, BS * BS), BF16), pltpu.VMEM((128, BS * BS), BF16), pltpu.VMEM((2, 32, 128), F32),
        ],
        compiler_params=pltpu.CompilerParams(vmem_limit_bytes=LARGE),
        name="tile_pairs",
    )(me, tiles, swapped, turned, *got)


def place_kernel(i0, i1, i2, i3, t0, t1, t2, t3, o_ref, total):
    total[...] = jnp.zeros_like(total)
    for info, terms in ((i0, t0), (i1, t1), (i2, t2), (i3, t3)):
        for t in range(terms.shape[0]):
            at = info[2, t]
            total[at] += terms[t]
    o_ref[...] = total[...].reshape(o_ref.shape).astype(BF16)


def place(infos, terms):
    return pl.pallas_call(
        place_kernel,
        out_shape=jax.ShapeDtypeStruct((64, 16, 128), BF16),
        in_specs=[SMEM] * 4 + [VMEM] * 4,
        out_specs=VMEM,
        scratch_shapes=[pltpu.VMEM((128, 8, 128), F32)],
        compiler_params=pltpu.CompilerParams(vmem_limit_bytes=SMALL),
        name="place",
    )(*infos, *terms)


def sum_kernel(s_ref, o_ref):
    o_ref[...] = jnp.sum(s_ref[...].astype(F32), axis=0)


def finish_kernel(me_ref, p0, p1, p2, p3, o_ref, whole):
    me = me_ref[0]
    for k, ref in enumerate((p0, p1, p2, p3)):
        x = (me - k + NX) & 3
        for aux in range(AUX):
            whole[aux, x] = ref[8 * aux:8 * aux + 8]
    one, two = whole[0].reshape(32, 128), whole[1].reshape(32, 128)
    low = low_lanes(32)
    o_ref[:32, :] = jnp.where(low, one, pltpu.roll(two, BS, 1))
    o_ref[32:, :] = jnp.where(low, pltpu.roll(one, BS, 1), two)


def shards(tiles, tile_dest, tile_aux, tile_row, tile_col, green_occ, green_virt):
    count = tiles.shape[0]
    x = lax.axis_index("x")
    me = x.reshape(1)
    info = jnp.stack([tile_row, tile_col, tile_dest * AUX + tile_aux])
    infos = [info] + [shift(info, k) for k in range(1, NX)]

    with jax.named_scope("gather_rows"):
        own = pl.pallas_call(
            rows_kernel,
            out_shape=jax.ShapeDtypeStruct((32, BS, 128), BF16),
            in_specs=[VMEM] * 2,
            out_specs=VMEM,
            scratch_shapes=[pltpu.VMEM((BS, 128), F32)],
            compiler_params=pltpu.CompilerParams(vmem_limit_bytes=SMALL),
            name="rows",
        )(green_occ, green_virt)
        rows = lax.all_to_all(own, ZHL, 0, 0)
    swapped, turned, hot = prep(infos, tiles)
    rows, hot = lax.optimization_barrier((rows, hot))
    other = lax.ppermute(rows, "c", [(0, 1), (1, 0)])

    with jax.named_scope("pick_blocks"):
        picked = pl.pallas_call(
            pick_kernel,
            out_shape=[jax.ShapeDtypeStruct((2, 2, 4, 2 * count, 128), BF16)] * NX,
            in_specs=[SMEM] + [VMEM] * 3,
            out_specs=[VMEM] * NX,
            compiler_params=pltpu.CompilerParams(vmem_limit_bytes=SMALL),
            name="pick",
        )(lax.axis_index("c").reshape(1), hot, rows, other)
        got = [picked[0]] + [shift(picked[NX - k], k) for k in range(1, NX)]

    quarters = tile_pairs(me, tiles, swapped, turned, got)

    with jax.named_scope("owners"):
        terms = [quarters[0]] + [shift(quarters[k], k) for k in range(1, NX)]
        spread = lax.all_to_all(place(infos, terms), TENS, 0, 0)
        owned = pl.pallas_call(
            sum_kernel, out_shape=jax.ShapeDtypeStruct((16, 128), F32), in_specs=[VMEM], out_specs=VMEM,
            compiler_params=pltpu.CompilerParams(vmem_limit_bytes=SMALL), name="sum",
        )(spread)
        parts = [owned] + [shift(owned, k) for k in range(1, NX)]
        out = pl.pallas_call(
            finish_kernel,
            out_shape=jax.ShapeDtypeStruct((BS, AUX * BS), F32),
            in_specs=[SMEM] + [VMEM] * 4,
            out_specs=pl.BlockSpec((BS, AUX * BS), lambda: (0, 0)),
            scratch_shapes=[pltpu.VMEM((AUX, NX, 8, 128), F32)],
            compiler_params=pltpu.CompilerParams(vmem_limit_bytes=SMALL),
            name="finish",
        )(me, *parts)
        return out.T


def solution(mesh):
    fine = Mesh(mesh.devices.reshape(8, 2, 2, 2, 4), ALL)
    return jax.shard_map(
        shards,
        mesh=fine,
        in_specs=(P(ALL, None, None), P(ALL), P(ALL), P(ALL), P(ALL), P(ALL, None), P(ALL, None)),
        out_specs=P(TENS, None),
        check_vma=False,
    )
```

```python
import jax
import jax.numpy as jnp
from jax import lax
from jax.experimental import pallas as pl
from jax.experimental.pallas import tpu as pltpu
from jax.sharding import Mesh, PartitionSpec as P

BS = 64
NA = 16
AUX = 2
ZH = ("z", "h")
ZHL = ("z", "h", "l")
LCX = ("l", "c", "x")
TENS = ("z", "h", "l", "c")
ALL = ("z", "h", "l", "c", "x")
NX = 4
NG = 16
F32, BF16 = jnp.float32, jnp.bfloat16
VMEM = pl.BlockSpec(memory_space=pltpu.VMEM)
SMEM = pl.BlockSpec(memory_space=pltpu.SMEM)
LARGE, MIDDLE, SMALL = 58 * 1024 * 1024, 52 * 1024 * 1024, 12 * 1024 * 1024
PITCH = 65


def shift(values, k):
    return lax.ppermute(values, "x", [(i, (i + k) % NX) for i in range(NX)])


def low_lanes(rows):
    return lax.broadcasted_iota(jnp.int32, (rows, 128), 1) < BS


def rows_kernel(occ_ref, virt_ref, o_ref, scr):
    for arr, ref in enumerate((occ_ref, virt_ref)):
        values = ref[...].astype(F32)
        for i in range(4):
            for pair in range(8):
                at = (arr * 4 + i) * 8 + pair
                scr[at:at + 1, :] = values[i:i + 1, pair * 128:pair * 128 + 128]
    block = scr[...].astype(BF16)
    for peer in range(o_ref.shape[0]):
        o_ref[peer] = block


def wants_kernel(row_ref, col_ref, dest_ref, aux_ref, o_ref):
    at = lax.broadcasted_iota(jnp.int32, (8, 128), 0)
    for j in range(3):
        found = jnp.zeros((8, 128), jnp.int32)
        for t in range(8):
            value = row_ref[t] if j == 0 else col_ref[t] if j == 1 else dest_ref[t] * AUX + aux_ref[t]
            found = jnp.where(at == t, value, found)
        o_ref[j] = found


def prep_kernel(t_ref, sw_ref, tr_ref, scr):
    for s in range(16):
        cut = slice(s * 256, s * 256 + 256)
        turned = jnp.concatenate([t_ref[0, :, cut], t_ref[1, :, cut]], axis=0).T
        for k in range(4):
            at = (4 * s + k) * PITCH
            scr[at:at + BS, :] = turned[k * BS:k * BS + BS].astype(F32)
        tr_ref[0, cut, :] = turned.astype(BF16)
    for s in range(16):
        cut = slice(s * 256, s * 256 + 256)
        rows = jnp.concatenate([scr[pl.ds(4 * s + k, BS, stride=PITCH), :] for k in range(4)], axis=0)
        back = rows.astype(BF16).T
        sw_ref[0, :, cut] = back[:BS]
        sw_ref[1, :, cut] = back[BS:]


def prep(tiles):
    count = tiles.shape[0]
    spec = pl.BlockSpec((2, BS, BS * BS), lambda i: (i, 0, 0))
    return pl.pallas_call(
        prep_kernel,
        grid=(count // 2,),
        out_shape=(
            jax.ShapeDtypeStruct(tiles.shape, BF16),
            jax.ShapeDtypeStruct((count // 2, BS * BS, 128), BF16),
        ),
        in_specs=[spec],
        out_specs=(spec, pl.BlockSpec((1, BS * BS, 128), lambda i: (i, 0, 0))),
        scratch_shapes=[pltpu.VMEM((BS * PITCH, 128), F32)],
        cost_estimate=pl.CostEstimate(flops=9_000_000_000, bytes_accessed=6 * tiles.size, transcendentals=0),
        compiler_params=pltpu.CompilerParams(vmem_limit_bytes=LARGE),
        name="prep",
    )(tiles)


def pick_kernel(core_ref, w0, w1, w2, w3, own_ref, other_ref, o0, o1, o2, o3):
    core = core_ref[0]
    row, col = (jnp.concatenate([w[j] for w in (w0, w1, w2, w3)], axis=0) for j in range(2))
    lane = lax.broadcasted_iota(jnp.int32, (32, 128), 1)
    low = low_lanes(32)
    hots = []
    for arr, first in enumerate((row, col)):
        hot = []
        for q in range(2):
            second = first if q == 0 else (col if arr == 0 else row)
            for odd in range(2):
                for i in range(2):
                    key = jnp.where((second & 1) == odd, first * 16 + i * 8 + (second >> 1), -1)
                    hot.append(jnp.concatenate([
                        jnp.where(lane == key, 1.0, 0.0).astype(BF16),
                        jnp.where(lane + 128 == key, 1.0, 0.0).astype(BF16),
                    ], axis=1))
        hots.append(jnp.concatenate(hot, axis=0))
    for side, ref in ((core, own_ref), (1 - core, other_ref)):
        for l in range(2):
            for ih in range(2):
                got = []
                for arr in range(2):
                    start = (arr * 2 + ih) * 16
                    table = jnp.concatenate([ref[2 * b + l, start:start + 16, :] for b in range(NA)], axis=0)
                    got.append(jnp.dot(hots[arr], table, preferred_element_type=F32))
                for il in range(2):
                    found = []
                    for arr in range(2):
                        g = [got[arr][(k * 2 + il) * 32:(k * 2 + il) * 32 + 32] for k in range(4)]
                        left = g[0] + pltpu.roll(g[1], BS, 1)
                        right = pltpu.roll(g[2], BS, 1) + g[3]
                        found.append(jnp.where(low, left, right))
                    for k, o_ref in enumerate((o0, o1, o2, o3)):
                        cut = slice(k * 8, k * 8 + 8)
                        o_ref[l, side, ih * 2 + il] = jnp.concatenate([f[cut] for f in found], axis=0).astype(BF16)


def tile_kernel(me_ref, t_ref, sw_ref, tr_ref, wants_ref, g0, g1, g2, g3, o_ref, gscr, us, ws, ys, zs, pk):
    step = pl.program_id(0)

    @pl.when(step == 0)
    def _():
        for k, ref in enumerate((g0, g1, g2, g3)):
            first = ((me_ref[0] - k + NX) & 3) * 4
            for l in range(2):
                for c in range(2):
                    for i in range(4):
                        at = pl.multiple_of((first + (l * 32 + c * 16 + i)) * 24, 8)
                        gscr[pl.ds(at, 16), :] = ref[l, c, i].astype(F32)

    low = low_lanes(BS)

    def blocks_t(arr, u):
        rows = gscr[pl.ds(arr * 8 + step * 2 + u, BS, stride=24), :]
        turned = jnp.concatenate([rows, rows], axis=0).T
        return turned[:BS], turned[BS:]

    def two(b):
        return jnp.concatenate([jnp.where(low, b, 0.0), jnp.where(low, 0.0, b)], axis=0).astype(BF16)

    def four(b):
        pair = two(b)
        none = jnp.zeros((128, 128), BF16)
        return jnp.concatenate([jnp.concatenate([pair, none], axis=1), jnp.concatenate([none, pair], axis=1)], axis=0)

    (cc0, cr0), (cc1, cr1) = blocks_t(1, 0), blocks_t(1, 1)
    virt = jnp.concatenate([
        jnp.concatenate([two(cc0), two(cc1)], axis=1),
        jnp.concatenate([two(cr0), two(cr1)], axis=1),
    ], axis=0)
    low128 = low_lanes(128)
    zero = jnp.zeros((128, 128), BF16)
    for s in range(16):
        a = tr_ref[0, s * 256:s * 256 + 128, :]
        b = tr_ref[0, s * 256 + 128:s * 256 + 256, :]
        rhs = jnp.concatenate([
            jnp.concatenate([jnp.where(low128, a, zero), jnp.where(low128, b, zero)], axis=1),
            jnp.concatenate([jnp.where(low128, zero, a), jnp.where(low128, zero, b)], axis=1),
        ], axis=0)
        out = jnp.dot(virt, rhs, preferred_element_type=F32)
        for ref, first in ((us, 0), (ws, 128)):
            for k in range(4):
                at, row, lane = (4 * s + k) * PITCH, first + (k % 2) * BS, (k // 2) * 128
                ref[at:at + BS, :] = out[row:row + BS, lane:lane + 128]
    for u in range(2):
        same, cross = blocks_t(0, u)
        for ref, dest, block in ((sw_ref, ys, same), (t_ref, zs, cross)):
            rows = jnp.concatenate([ref[u, :, s * 256:s * 256 + 256] for s in range(16)], axis=0)
            out = jnp.dot(rows, four(block), preferred_element_type=F32).astype(BF16)
            for s in range(16):
                dest[u * BS:u * BS + BS, s * 256:s * 256 + 256] = out[s * BS:s * BS + BS]
    acc = jnp.zeros((128, 128), F32)
    for left, right in ((ys, us), (zs, ws)):
        for s in range(16):
            rows = jnp.concatenate([right[pl.ds(4 * s + k, BS, stride=PITCH), :] for k in range(4)], axis=0)
            acc += jnp.dot(left[:, s * 256:s * 256 + 256], rows.astype(BF16), preferred_element_type=F32)
    acc = acc * (1.0 / BS)
    low32 = low_lanes(32)
    packed = (
        jnp.where(low32, acc[:32], pltpu.roll(acc[32:64], BS, 1)),
        jnp.where(low32, pltpu.roll(acc[64:96], BS, 1), acc[96:]),
    )
    for u in range(2):
        pk[pl.ds(pl.multiple_of((step * 2 + u) * 40, 8), 32), :] = packed[u]

    @pl.when(step == pl.num_programs(0) - 1)
    def _():
        target = wants_ref[2].astype(F32)
        for peer in range(NG):
            for half in range(2):
                o_ref[peer, half * 8:half * 8 + 8] = pk[pl.ds(2 * peer + half, 8, stride=40), :]
            o_ref[peer, 16:24] = target


def tile_pairs(me, tiles, swapped, turned, wants, got):
    count = tiles.shape[0]
    tile = pl.BlockSpec((2, BS, BS * BS), lambda i: (i, 0, 0))
    return pl.pallas_call(
        tile_kernel,
        grid=(count // 2,),
        out_shape=jax.ShapeDtypeStruct((NG, 3 * count, 128), F32),
        in_specs=[SMEM, tile, tile, pl.BlockSpec((1, BS * BS, 128), lambda i: (i, 0, 0))] + [VMEM] * 5,
        out_specs=pl.BlockSpec((NG, 3 * count, 128), lambda i: (0, 0, 0)),
        scratch_shapes=[
            pltpu.VMEM((BS * 24, 128), F32), pltpu.VMEM((BS * PITCH, 128), F32), pltpu.VMEM((BS * PITCH, 128), F32),
            pltpu.VMEM((128, BS * BS), BF16), pltpu.VMEM((128, BS * BS), BF16), pltpu.VMEM((count * 40, 128), F32),
        ],
        compiler_params=pltpu.CompilerParams(vmem_limit_bytes=MIDDLE),
        name="tile_pairs",
    )(me, tiles, swapped, turned, wants, *got)


def place_kernel(t_ref, o_ref):
    target = t_ref[:, 16:24, :].reshape(128, 128).astype(jnp.int32)
    lane = lax.broadcasted_iota(jnp.int32, (128, 128), 1)
    hot = jnp.where(lane == target, 1.0, 0.0).T.astype(BF16)
    dense = []
    for half in range(2):
        terms = t_ref[:, half * 8:half * 8 + 8, :].reshape(128, 128)
        high = terms.astype(BF16)
        rest = (terms - high.astype(F32)).astype(BF16)
        dense.append(jnp.dot(hot, high, preferred_element_type=F32) + jnp.dot(hot, rest, preferred_element_type=F32))
    for peer in range(NG):
        o_ref[peer] = jnp.concatenate([d[peer * 8:peer * 8 + 8] for d in dense], axis=0).astype(BF16)


def sum_kernel(s_ref, o_ref):
    total = jnp.sum(s_ref[...].astype(F32), axis=0)
    none = jnp.zeros((4, 128), F32)
    for peer in range(NG):
        at = (peer // 4) * 2
        rows = [total[half * 8 + at + aux:half * 8 + at + aux + 1] for aux in range(AUX) for half in range(2)]
        o_ref[peer] = jnp.concatenate(rows + [none], axis=0)


def finish_kernel(p_ref, o_ref, whole):
    for aux in range(AUX):
        for peer in range(NG):
            whole[aux, 2 * peer:2 * peer + 2, :] = p_ref[peer, 2 * aux:2 * aux + 2, :]
    one, two = whole[0], whole[1]
    low = low_lanes(32)
    o_ref[:32, :] = jnp.where(low, one, pltpu.roll(two, BS, 1))
    o_ref[32:, :] = jnp.where(low, pltpu.roll(one, BS, 1), two)


def call(kernel, name, out, *args, spaces=None, limit=SMALL, **more):
    return pl.pallas_call(
        kernel,
        out_shape=[jax.ShapeDtypeStruct(*s) for s in out] if isinstance(out, list) else jax.ShapeDtypeStruct(*out),
        in_specs=spaces or [VMEM] * len(args),
        compiler_params=pltpu.CompilerParams(vmem_limit_bytes=limit),
        name=name,
        **more,
    )(*args)


def shards(tiles, tile_dest, tile_aux, tile_row, tile_col, green_occ, green_virt):
    me = lax.axis_index("x").reshape(1)
    own = call(rows_kernel, "rows", ((32, BS, 128), BF16), green_occ, green_virt, limit=LARGE,
               out_specs=VMEM, scratch_shapes=[pltpu.VMEM((BS, 128), F32)])
    rows = lax.all_to_all(own, ZHL, 0, 0)
    tile_row, own = lax.optimization_barrier((tile_row, own))
    wants = call(wants_kernel, "wants", ((3, 8, 128), jnp.int32), tile_row, tile_col, tile_dest, tile_aux,
                 spaces=[SMEM] * 4, limit=LARGE, out_specs=VMEM)
    asked = [wants] + [shift(wants, k) for k in range(1, NX)]
    swapped, turned = prep(tiles)
    rows, turned, asked = lax.optimization_barrier((rows, turned, asked))
    other = lax.ppermute(rows, "c", [(0, 1), (1, 0)])
    picked = call(pick_kernel, "pick", [((2, 2, 4, 16, 128), BF16)] * NX, lax.axis_index("c").reshape(1), *asked, rows, other,
                  spaces=[SMEM] + [VMEM] * 6, out_specs=[VMEM] * NX)
    got = [picked[0]] + [shift(picked[NX - k], k) for k in range(1, NX)]
    pieces = tile_pairs(me, tiles, swapped, turned, wants, got)
    terms = lax.all_to_all(pieces, LCX, 0, 0)
    dense = call(place_kernel, "place", ((NG, 16, 128), BF16), terms, out_specs=VMEM)
    spread = lax.all_to_all(dense, ZH, 0, 0)
    owned = call(sum_kernel, "sum", ((NG, 8, 128), F32), spread, out_specs=VMEM)
    parts = lax.all_to_all(owned, LCX, 0, 0)
    out = call(finish_kernel, "finish", ((BS, AUX * BS), F32), parts,
               out_specs=pl.BlockSpec((BS, AUX * BS), lambda: (0, 0)),
               scratch_shapes=[pltpu.VMEM((AUX, 32, 128), F32)])
    return out.T


def solution(mesh):
    fine = Mesh(mesh.devices.reshape(8, 2, 2, 2, 4), ALL)
    return jax.shard_map(
        shards,
        mesh=fine,
        in_specs=(P(ALL, None, None), P(ALL), P(ALL), P(ALL), P(ALL), P(ALL, None), P(ALL, None)),
        out_specs=P(TENS, None),
        check_vma=False,
    )
```

```python
import jax
import jax.numpy as jnp
from jax import lax
from jax.experimental import pallas as pl
from jax.experimental.pallas import tpu as pltpu
from jax.sharding import Mesh, PartitionSpec as P

BS = 64
NA = 16
AUX = 2
ZHL = ("z", "h", "l")
CX = ("c", "x")
TENS = ("z", "h", "l", "c")
ALL = ("z", "h", "l", "c", "x")
NX = 4
NG = 8
F32, BF16 = jnp.float32, jnp.bfloat16
VMEM = pl.BlockSpec(memory_space=pltpu.VMEM)
SMEM = pl.BlockSpec(memory_space=pltpu.SMEM)
LARGE, MIDDLE, SMALL = 58 * 1024 * 1024, 52 * 1024 * 1024, 12 * 1024 * 1024
PITCH = 65


def shift(values, k):
    return lax.ppermute(values, "x", [(i, (i + k) % NX) for i in range(NX)])


def low_lanes(rows):
    return lax.broadcasted_iota(jnp.int32, (rows, 128), 1) < BS


def rows_kernel(row_ref, col_ref, dest_ref, aux_ref, occ_ref, virt_ref, o_ref, wants_ref, scr):
    at = lax.broadcasted_iota(jnp.int32, (8, 128), 0)
    for j in range(3):
        found = jnp.zeros((8, 128), jnp.int32)
        for t in range(8):
            value = row_ref[t] if j == 0 else col_ref[t] if j == 1 else dest_ref[t] * AUX + aux_ref[t]
            found = jnp.where(at == t, value, found)
        wants_ref[j] = found
    for arr, ref in enumerate((occ_ref, virt_ref)):
        values = ref[...].astype(F32)
        for i in range(4):
            for pair in range(8):
                at = (arr * 4 + i) * 8 + pair
                scr[at:at + 1, :] = values[i:i + 1, pair * 128:pair * 128 + 128]
    block = scr[...].astype(BF16)
    for peer in range(o_ref.shape[0]):
        o_ref[peer] = block


def prep_kernel(t_ref, sw_ref, scr):
    for s in range(16):
        cut = slice(s * 256, s * 256 + 256)
        turned = jnp.concatenate([t_ref[0, :, cut], t_ref[1, :, cut]], axis=0).T
        for k in range(4):
            at = (4 * s + k) * PITCH
            scr[at:at + BS, :] = turned[k * BS:k * BS + BS].astype(F32)
    for s in range(16):
        cut = slice(s * 256, s * 256 + 256)
        rows = jnp.concatenate([scr[pl.ds(4 * s + k, BS, stride=PITCH), :] for k in range(4)], axis=0)
        back = rows.astype(BF16).T
        sw_ref[0, :, cut] = back[:BS]
        sw_ref[1, :, cut] = back[BS:]


def prep(tiles):
    count = tiles.shape[0]
    spec = pl.BlockSpec((2, BS, BS * BS), lambda i: (i, 0, 0))
    return pl.pallas_call(
        prep_kernel,
        grid=(count // 2,),
        out_shape=jax.ShapeDtypeStruct(tiles.shape, BF16),
        in_specs=[spec],
        out_specs=spec,
        scratch_shapes=[pltpu.VMEM((BS * PITCH, 128), F32)],
        cost_estimate=pl.CostEstimate(flops=9_000_000_000, bytes_accessed=4 * tiles.size, transcendentals=0),
        compiler_params=pltpu.CompilerParams(vmem_limit_bytes=LARGE),
        name="prep",
    )(tiles)


def pick_kernel(core_ref, w0, w1, w2, w3, own_ref, other_ref, o0, o1, o2, o3):
    core = core_ref[0]
    row, col = (jnp.concatenate([w[j] for w in (w0, w1, w2, w3)], axis=0) for j in range(2))
    lane = lax.broadcasted_iota(jnp.int32, (32, 128), 1)
    low = low_lanes(32)
    hots = []
    for arr, first in enumerate((row, col)):
        hot = []
        for q in range(2):
            second = first if q == 0 else (col if arr == 0 else row)
            for odd in range(2):
                for i in range(2):
                    key = jnp.where((second & 1) == odd, first * 16 + i * 8 + (second >> 1), -1)
                    hot.append(jnp.concatenate([
                        jnp.where(lane == key, 1.0, 0.0).astype(BF16),
                        jnp.where(lane + 128 == key, 1.0, 0.0).astype(BF16),
                    ], axis=1))
        hots.append(jnp.concatenate(hot, axis=0))
    for side, ref in ((core, own_ref), (1 - core, other_ref)):
        for l in range(2):
            for ih in range(2):
                got = []
                for arr in range(2):
                    start = (arr * 2 + ih) * 16
                    table = jnp.concatenate([ref[2 * b + l, start:start + 16, :] for b in range(NA)], axis=0)
                    got.append(jnp.dot(hots[arr], table, preferred_element_type=F32))
                for il in range(2):
                    found = []
                    for arr in range(2):
                        g = [got[arr][(k * 2 + il) * 32:(k * 2 + il) * 32 + 32] for k in range(4)]
                        left = g[0] + pltpu.roll(g[1], BS, 1)
                        right = pltpu.roll(g[2], BS, 1) + g[3]
                        found.append(jnp.where(low, left, right))
                    for k, o_ref in enumerate((o0, o1, o2, o3)):
                        cut = slice(k * 8, k * 8 + 8)
                        o_ref[l, side, ih * 2 + il] = jnp.concatenate([f[cut] for f in found], axis=0).astype(BF16)


def tile_kernel(me_ref, t_ref, sw_ref, wants_ref, g0, g1, g2, g3, o_ref, gscr, us, ws, ys, zs, pk):
    step = pl.program_id(0)

    @pl.when(step == 0)
    def _():
        for k, ref in enumerate((g0, g1, g2, g3)):
            first = ((me_ref[0] - k + NX) & 3) * 4
            for l in range(2):
                for c in range(2):
                    for i in range(4):
                        at = pl.multiple_of((first + (l * 32 + c * 16 + i)) * 24, 8)
                        gscr[pl.ds(at, 16), :] = ref[l, c, i].astype(F32)

    low = low_lanes(BS)

    def blocks_t(arr, u):
        rows = gscr[pl.ds(arr * 8 + step * 2 + u, BS, stride=24), :]
        turned = jnp.concatenate([rows, rows], axis=0).T
        return turned[:BS], turned[BS:]

    def two(b):
        return jnp.concatenate([jnp.where(low, b, 0.0), jnp.where(low, 0.0, b)], axis=0).astype(BF16)

    def four(b):
        pair = two(b)
        none = jnp.zeros((128, 128), BF16)
        return jnp.concatenate([jnp.concatenate([pair, none], axis=1), jnp.concatenate([none, pair], axis=1)], axis=0)

    (cc0, cr0), (cc1, cr1) = blocks_t(1, 0), blocks_t(1, 1)
    virt = jnp.concatenate([
        jnp.concatenate([two(cc0), two(cc1)], axis=1),
        jnp.concatenate([two(cr0), two(cr1)], axis=1),
    ], axis=0)
    low128 = low_lanes(128)
    zero = jnp.zeros((128, 128), BF16)
    for s in range(16):
        cut = slice(s * 256, s * 256 + 256)
        turned = jnp.concatenate([t_ref[0, :, cut], t_ref[1, :, cut]], axis=0).T
        a, b = turned[:128], turned[128:]
        rhs = jnp.concatenate([
            jnp.concatenate([jnp.where(low128, a, zero), jnp.where(low128, b, zero)], axis=1),
            jnp.concatenate([jnp.where(low128, zero, a), jnp.where(low128, zero, b)], axis=1),
        ], axis=0)
        out = jnp.dot(virt, rhs, preferred_element_type=F32)
        for ref, first in ((us, 0), (ws, 128)):
            for k in range(4):
                at, row, lane = (4 * s + k) * PITCH, first + (k % 2) * BS, (k // 2) * 128
                ref[at:at + BS, :] = out[row:row + BS, lane:lane + 128]
    for u in range(2):
        same, cross = blocks_t(0, u)
        for ref, dest, block in ((sw_ref, ys, same), (t_ref, zs, cross)):
            rows = jnp.concatenate([ref[u, :, s * 256:s * 256 + 256] for s in range(16)], axis=0)
            out = jnp.dot(rows, four(block), preferred_element_type=F32).astype(BF16)
            for s in range(16):
                dest[u * BS:u * BS + BS, s * 256:s * 256 + 256] = out[s * BS:s * BS + BS]
    acc = jnp.zeros((128, 128), F32)
    for left, right in ((ys, us), (zs, ws)):
        for s in range(16):
            rows = jnp.concatenate([right[pl.ds(4 * s + k, BS, stride=PITCH), :] for k in range(4)], axis=0)
            acc += jnp.dot(left[:, s * 256:s * 256 + 256], rows.astype(BF16), preferred_element_type=F32)
    acc = acc * (1.0 / BS)
    low32 = low_lanes(32)
    packed = (
        jnp.where(low32, acc[:32], pltpu.roll(acc[32:64], BS, 1)),
        jnp.where(low32, pltpu.roll(acc[64:96], BS, 1), acc[96:]),
    )
    for u in range(2):
        pk[pl.ds(pl.multiple_of((step * 2 + u) * 40, 8), 32), :] = packed[u]

    @pl.when(step == pl.num_programs(0) - 1)
    def _():
        target = wants_ref[2].astype(F32)
        for peer in range(NG):
            for r in range(4):
                o_ref[peer, r * 8:r * 8 + 8] = pk[pl.ds(4 * peer + r, 8, stride=40), :]
            o_ref[peer, 32:40] = target


def tile_pairs(me, tiles, swapped, wants, got):
    count = tiles.shape[0]
    tile = pl.BlockSpec((2, BS, BS * BS), lambda i: (i, 0, 0))
    return pl.pallas_call(
        tile_kernel,
        grid=(count // 2,),
        out_shape=jax.ShapeDtypeStruct((NG, 5 * count, 128), F32),
        in_specs=[SMEM, tile, tile] + [VMEM] * 5,
        out_specs=pl.BlockSpec((NG, 5 * count, 128), lambda i: (0, 0, 0)),
        scratch_shapes=[
            pltpu.VMEM((BS * 24, 128), F32), pltpu.VMEM((BS * PITCH, 128), F32), pltpu.VMEM((BS * PITCH, 128), F32),
            pltpu.VMEM((128, BS * BS), BF16), pltpu.VMEM((128, BS * BS), BF16), pltpu.VMEM((count * 40, 128), F32),
        ],
        compiler_params=pltpu.CompilerParams(vmem_limit_bytes=MIDDLE),
        name="tile_pairs",
    )(me, tiles, swapped, wants, *got)


def place_kernel(t_ref, o_ref):
    target = t_ref[:, 32:40, :].reshape(64, 128)
    target = jnp.concatenate([target, target], axis=0).T.astype(jnp.int32)
    lane = lax.broadcasted_iota(jnp.int32, (128, 128), 1)
    terms = jnp.concatenate([t_ref[:, r * 8:r * 8 + 8, :].reshape(64, 128) for r in range(4)], axis=0)
    high = terms.astype(BF16)
    rest = (terms - high.astype(F32)).astype(BF16)
    for part in range(4):
        row = lax.broadcasted_iota(jnp.int32, (128, 128), 0) + part * 128
        here = ((row >> 4) == (target >> 2)) & ((row & 3) == (target & 3))
        hot = jnp.concatenate([
            jnp.where(here & (((row >> 2) & 3) == (lane >> 6) + 2 * half), 1.0, 0.0).astype(BF16) for half in range(2)
        ], axis=1)
        dense = jnp.dot(hot, high, preferred_element_type=F32) + jnp.dot(hot, rest, preferred_element_type=F32)
        o_ref[part * 8:part * 8 + 8] = dense.astype(BF16).reshape(8, 16, 128)


def sum_kernel(s_ref, o_ref):
    total = jnp.sum(s_ref[...].astype(F32), axis=0)
    for core in range(2):
        at = [r * 4 + core * 2 + aux for aux in range(AUX) for r in range(4)]
        rows = jnp.concatenate([total[i:i + 1] for i in at], axis=0)
        for x in range(NX):
            o_ref[core * NX + x] = rows


def finish_kernel(p_ref, o_ref, whole):
    for aux in range(AUX):
        for peer in range(NG):
            whole[aux, 4 * peer:4 * peer + 4, :] = p_ref[peer, 4 * aux:4 * aux + 4, :]
    one, two = whole[0], whole[1]
    low = low_lanes(32)
    o_ref[:32, :] = jnp.where(low, one, pltpu.roll(two, BS, 1))
    o_ref[32:, :] = jnp.where(low, pltpu.roll(one, BS, 1), two)


def call(kernel, name, out, *args, spaces=None, limit=SMALL, **more):
    return pl.pallas_call(
        kernel,
        out_shape=[jax.ShapeDtypeStruct(*s) for s in out] if isinstance(out, list) else jax.ShapeDtypeStruct(*out),
        in_specs=spaces or [VMEM] * len(args),
        compiler_params=pltpu.CompilerParams(vmem_limit_bytes=limit),
        name=name,
        **more,
    )(*args)


def shards(tiles, tile_dest, tile_aux, tile_row, tile_col, green_occ, green_virt):
    me = lax.axis_index("x").reshape(1)
    own, wants = call(rows_kernel, "rows", [((32, BS, 128), BF16), ((3, 8, 128), jnp.int32)],
                      tile_row, tile_col, tile_dest, tile_aux, green_occ, green_virt,
                      spaces=[SMEM] * 4 + [VMEM] * 2, limit=LARGE, out_specs=[VMEM] * 2, scratch_shapes=[pltpu.VMEM((BS, 128), F32)])
    rows = lax.all_to_all(own, ZHL, 0, 0)
    asked = [wants] + [shift(wants, k) for k in range(1, NX)]
    swapped = prep(tiles)
    rows, swapped, asked = lax.optimization_barrier((rows, swapped, asked))
    other = lax.ppermute(rows, "c", [(0, 1), (1, 0)])
    picked = call(pick_kernel, "pick", [((2, 2, 4, 16, 128), BF16)] * NX, lax.axis_index("c").reshape(1), *asked, rows, other,
                  spaces=[SMEM] + [VMEM] * 6, out_specs=[VMEM] * NX)
    got = [picked[0]] + [shift(picked[NX - k], k) for k in range(1, NX)]
    pieces = tile_pairs(me, tiles, swapped, wants, got)
    terms = lax.all_to_all(pieces, CX, 0, 0)
    dense = call(place_kernel, "place", ((32, 16, 128), BF16), terms, out_specs=VMEM)
    spread = lax.all_to_all(dense, ZHL, 0, 0)
    owned = call(sum_kernel, "sum", ((NG, 8, 128), F32), spread, out_specs=VMEM)
    parts = lax.all_to_all(owned, CX, 0, 0)
    out = call(finish_kernel, "finish", ((BS, AUX * BS), F32), parts,
               out_specs=pl.BlockSpec((BS, AUX * BS), lambda: (0, 0)),
               scratch_shapes=[pltpu.VMEM((AUX, 32, 128), F32)])
    return out.T


def solution(mesh):
    fine = Mesh(mesh.devices.reshape(8, 2, 2, 2, 4), ALL)
    return jax.shard_map(
        shards,
        mesh=fine,
        in_specs=(P(ALL, None, None), P(ALL), P(ALL), P(ALL), P(ALL), P(ALL, None), P(ALL, None)),
        out_specs=P(TENS, None),
        check_vma=False,
    )
```

```python
import jax
import jax.numpy as jnp
from jax import lax
from jax.experimental import pallas as pl
from jax.experimental.pallas import tpu as pltpu
from jax.sharding import Mesh, PartitionSpec as P

BS = 64
NA = 16
AUX = 2
ZHL = ("z", "h", "l")
HL = ("h", "l")
CX = ("c", "x")
TENS = ("z", "h", "l", "c")
ALL = ("z", "h", "l", "c", "x")
NX = NY = 4
NG = 8
F32, BF16 = jnp.float32, jnp.bfloat16
VMEM = pl.BlockSpec(memory_space=pltpu.VMEM)
SMEM = pl.BlockSpec(memory_space=pltpu.SMEM)
LARGE, MIDDLE, SMALL = 58 * 1024 * 1024, 52 * 1024 * 1024, 12 * 1024 * 1024
PITCH = 65


def shift(values, k):
    return lax.ppermute(values, "x", [(i, (i + k) % NX) for i in range(NX)])


def low_lanes(rows):
    return lax.broadcasted_iota(jnp.int32, (rows, 128), 1) < BS


def rows_kernel(row_ref, col_ref, dest_ref, aux_ref, occ_ref, virt_ref, o_ref, wants_ref, scr):
    at = lax.broadcasted_iota(jnp.int32, (8, 128), 0)
    for j in range(3):
        found = jnp.zeros((8, 128), jnp.int32)
        for t in range(8):
            value = row_ref[t] if j == 0 else col_ref[t] if j == 1 else dest_ref[t] * AUX + aux_ref[t]
            found = jnp.where(at == t, value, found)
        wants_ref[j] = found
    for arr, ref in enumerate((occ_ref, virt_ref)):
        values = ref[...].astype(F32)
        for i in range(4):
            for pair in range(8):
                at = (arr * 4 + i) * 8 + pair
                scr[at:at + 1, :] = values[i:i + 1, pair * 128:pair * 128 + 128]
    block = scr[...].astype(BF16)
    for peer in range(o_ref.shape[0]):
        o_ref[peer] = block


def prep_kernel(t_ref, sw_ref, scr):
    for s in range(16):
        cut = slice(s * 256, s * 256 + 256)
        turned = jnp.concatenate([t_ref[0, :, cut], t_ref[1, :, cut]], axis=0).T
        for k in range(4):
            at = (4 * s + k) * PITCH
            scr[at:at + BS, :] = turned[k * BS:k * BS + BS].astype(F32)
    for s in range(16):
        cut = slice(s * 256, s * 256 + 256)
        rows = jnp.concatenate([scr[pl.ds(4 * s + k, BS, stride=PITCH), :] for k in range(4)], axis=0)
        back = rows.astype(BF16).T
        sw_ref[0, :, cut] = back[:BS]
        sw_ref[1, :, cut] = back[BS:]


def prep(tiles):
    count = tiles.shape[0]
    spec = pl.BlockSpec((2, BS, BS * BS), lambda i: (i, 0, 0))
    return pl.pallas_call(
        prep_kernel,
        grid=(count // 2,),
        out_shape=jax.ShapeDtypeStruct(tiles.shape, BF16),
        in_specs=[spec],
        out_specs=spec,
        scratch_shapes=[pltpu.VMEM((BS * PITCH, 128), F32)],
        cost_estimate=pl.CostEstimate(flops=9_000_000_000, bytes_accessed=4 * tiles.size, transcendentals=0),
        compiler_params=pltpu.CompilerParams(vmem_limit_bytes=LARGE),
        name="prep",
    )(tiles)


def pick_kernel(core_ref, y_ref, w0, w1, w2, w3, *refs):
    pieces, (o0, o1, o2, o3, rows) = refs[:2 * NY], refs[2 * NY:]
    for k in range(NY):
        y = (y_ref[0] - k + NY) & 3
        rows[core_ref[0], y] = pieces[k][...]
        rows[1 - core_ref[0], y] = pieces[NY + k][...]
    row, col = (jnp.concatenate([w[j] for w in (w0, w1, w2, w3)], axis=0) for j in range(2))
    lane = lax.broadcasted_iota(jnp.int32, (32, 128), 1)
    low = low_lanes(32)
    hots = []
    for arr, first in enumerate((row, col)):
        hot = []
        for q in range(2):
            second = first if q == 0 else (col if arr == 0 else row)
            for odd in range(2):
                for i in range(2):
                    key = jnp.where((second & 1) == odd, first * 16 + i * 8 + (second >> 1), -1)
                    hot.append(jnp.concatenate([
                        jnp.where(lane == key, 1.0, 0.0).astype(BF16),
                        jnp.where(lane + 128 == key, 1.0, 0.0).astype(BF16),
                    ], axis=1))
        hots.append(jnp.concatenate(hot, axis=0))
    for side in range(2):
        for l in range(2):
            for ih in range(2):
                got = []
                for arr in range(2):
                    start = (arr * 2 + ih) * 16
                    table = jnp.concatenate([rows[side, 2 * (b % 2) + l, b // 2, start:start + 16, :] for b in range(NA)], axis=0)
                    got.append(jnp.dot(hots[arr], table, preferred_element_type=F32))
                for il in range(2):
                    found = []
                    for arr in range(2):
                        g = [got[arr][(k * 2 + il) * 32:(k * 2 + il) * 32 + 32] for k in range(4)]
                        left = g[0] + pltpu.roll(g[1], BS, 1)
                        right = pltpu.roll(g[2], BS, 1) + g[3]
                        found.append(jnp.where(low, left, right))
                    for k, o_ref in enumerate((o0, o1, o2, o3)):
                        cut = slice(k * 8, k * 8 + 8)
                        o_ref[l, side, ih * 2 + il] = jnp.concatenate([f[cut] for f in found], axis=0).astype(BF16)


def tile_kernel(me_ref, t_ref, sw_ref, wants_ref, g0, g1, g2, g3, o_ref, gscr, us, ws, ys, zs, pk):
    step = pl.program_id(0)

    @pl.when(step == 0)
    def _():
        for k, ref in enumerate((g0, g1, g2, g3)):
            first = ((me_ref[0] - k + NX) & 3) * 4
            for l in range(2):
                for c in range(2):
                    for i in range(4):
                        at = pl.multiple_of((first + (l * 32 + c * 16 + i)) * 24, 8)
                        gscr[pl.ds(at, 16), :] = ref[l, c, i].astype(F32)

    low = low_lanes(BS)

    def blocks_t(arr, u):
        rows = gscr[pl.ds(arr * 8 + step * 2 + u, BS, stride=24), :]
        turned = jnp.concatenate([rows, rows], axis=0).T
        return turned[:BS], turned[BS:]

    def two(b):
        return jnp.concatenate([jnp.where(low, b, 0.0), jnp.where(low, 0.0, b)], axis=0).astype(BF16)

    def four(b):
        pair = two(b)
        none = jnp.zeros((128, 128), BF16)
        return jnp.concatenate([jnp.concatenate([pair, none], axis=1), jnp.concatenate([none, pair], axis=1)], axis=0)

    (cc0, cr0), (cc1, cr1) = blocks_t(1, 0), blocks_t(1, 1)
    virt = jnp.concatenate([
        jnp.concatenate([two(cc0), two(cc1)], axis=1),
        jnp.concatenate([two(cr0), two(cr1)], axis=1),
    ], axis=0)
    low128 = low_lanes(128)
    zero = jnp.zeros((128, 128), BF16)
    for s in range(16):
        cut = slice(s * 256, s * 256 + 256)
        turned = jnp.concatenate([t_ref[0, :, cut], t_ref[1, :, cut]], axis=0).T
        a, b = turned[:128], turned[128:]
        rhs = jnp.concatenate([
            jnp.concatenate([jnp.where(low128, a, zero), jnp.where(low128, b, zero)], axis=1),
            jnp.concatenate([jnp.where(low128, zero, a), jnp.where(low128, zero, b)], axis=1),
        ], axis=0)
        out = jnp.dot(virt, rhs, preferred_element_type=F32)
        for ref, first in ((us, 0), (ws, 128)):
            for k in range(4):
                at, row, lane = (4 * s + k) * PITCH, first + (k % 2) * BS, (k // 2) * 128
                ref[at:at + BS, :] = out[row:row + BS, lane:lane + 128]
    for u in range(2):
        same, cross = blocks_t(0, u)
        for ref, dest, block in ((sw_ref, ys, same), (t_ref, zs, cross)):
            rows = jnp.concatenate([ref[u, :, s * 256:s * 256 + 256] for s in range(16)], axis=0)
            out = jnp.dot(rows, four(block), preferred_element_type=F32).astype(BF16)
            for s in range(16):
                dest[u * BS:u * BS + BS, s * 256:s * 256 + 256] = out[s * BS:s * BS + BS]
    acc = jnp.zeros((128, 128), F32)
    for left, right in ((ys, us), (zs, ws)):
        for s in range(16):
            rows = jnp.concatenate([right[pl.ds(4 * s + k, BS, stride=PITCH), :] for k in range(4)], axis=0)
            acc += jnp.dot(left[:, s * 256:s * 256 + 256], rows.astype(BF16), preferred_element_type=F32)
    acc = acc * (1.0 / BS)
    low32 = low_lanes(32)
    packed = (
        jnp.where(low32, acc[:32], pltpu.roll(acc[32:64], BS, 1)),
        jnp.where(low32, pltpu.roll(acc[64:96], BS, 1), acc[96:]),
    )
    for u in range(2):
        pk[pl.ds(pl.multiple_of((step * 2 + u) * 40, 8), 32), :] = packed[u]

    @pl.when(step == pl.num_programs(0) - 1)
    def _():
        target = wants_ref[2].astype(F32)
        for peer in range(NG):
            for r in range(4):
                o_ref[peer, r * 8:r * 8 + 8] = pk[pl.ds(4 * peer + r, 8, stride=40), :]
            o_ref[peer, 32:40] = target


def tile_pairs(me, tiles, swapped, wants, got):
    count = tiles.shape[0]
    tile = pl.BlockSpec((2, BS, BS * BS), lambda i: (i, 0, 0))
    return pl.pallas_call(
        tile_kernel,
        grid=(count // 2,),
        out_shape=jax.ShapeDtypeStruct((NG, 5 * count, 128), F32),
        in_specs=[SMEM, tile, tile] + [VMEM] * 5,
        out_specs=pl.BlockSpec((NG, 5 * count, 128), lambda i: (0, 0, 0)),
        scratch_shapes=[
            pltpu.VMEM((BS * 24, 128), F32), pltpu.VMEM((BS * PITCH, 128), F32), pltpu.VMEM((BS * PITCH, 128), F32),
            pltpu.VMEM((128, BS * BS), BF16), pltpu.VMEM((128, BS * BS), BF16), pltpu.VMEM((count * 40, 128), F32),
        ],
        compiler_params=pltpu.CompilerParams(vmem_limit_bytes=MIDDLE),
        name="tile_pairs",
    )(me, tiles, swapped, wants, *got)


def place_kernel(t_ref, o_ref):
    target = t_ref[:, 32:40, :].reshape(64, 128)
    target = jnp.concatenate([target, target], axis=0).T.astype(jnp.int32)
    lane = lax.broadcasted_iota(jnp.int32, (128, 128), 1)
    terms = jnp.concatenate([t_ref[:, r * 8:r * 8 + 8, :].reshape(64, 128) for r in range(4)], axis=0)
    high = terms.astype(BF16)
    rest = (terms - high.astype(F32)).astype(BF16)
    for part in range(4):
        row = lax.broadcasted_iota(jnp.int32, (128, 128), 0) + part * 128
        here = ((row >> 4) == (target >> 2)) & ((row & 3) == (target & 3))
        hot = jnp.concatenate([
            jnp.where(here & (((row >> 2) & 3) == (lane >> 6) + 2 * half), 1.0, 0.0).astype(BF16) for half in range(2)
        ], axis=1)
        dense = jnp.dot(hot, high, preferred_element_type=F32) + jnp.dot(hot, rest, preferred_element_type=F32)
        o_ref[part * 8:part * 8 + 8] = dense.astype(BF16).reshape(8, 16, 128)


def sum_kernel(s_ref, o_ref):
    total = jnp.sum(s_ref[...].astype(F32), axis=0)
    for core in range(2):
        at = [r * 4 + core * 2 + aux for aux in range(AUX) for r in range(4)]
        rows = jnp.concatenate([total[i:i + 1] for i in at], axis=0)
        for x in range(NX):
            o_ref[core * NX + x] = rows


def finish_kernel(p_ref, o_ref, whole):
    for aux in range(AUX):
        for peer in range(NG):
            whole[aux, 4 * peer:4 * peer + 4, :] = p_ref[peer, 4 * aux:4 * aux + 4, :]
    one, two = whole[0], whole[1]
    low = low_lanes(32)
    o_ref[:32, :] = jnp.where(low, one, pltpu.roll(two, BS, 1))
    o_ref[32:, :] = jnp.where(low, pltpu.roll(one, BS, 1), two)


def call(kernel, name, out, *args, spaces=None, limit=SMALL, **more):
    return pl.pallas_call(
        kernel,
        out_shape=[jax.ShapeDtypeStruct(*s) for s in out] if isinstance(out, list) else jax.ShapeDtypeStruct(*out),
        in_specs=spaces or [VMEM] * len(args),
        compiler_params=pltpu.CompilerParams(vmem_limit_bytes=limit),
        name=name,
        **more,
    )(*args)


def shards(tiles, tile_dest, tile_aux, tile_row, tile_col, green_occ, green_virt):
    me = lax.axis_index("x").reshape(1)
    own, wants = call(rows_kernel, "rows", [((8, BS, 128), BF16), ((3, 8, 128), jnp.int32)],
                      tile_row, tile_col, tile_dest, tile_aux, green_occ, green_virt,
                      spaces=[SMEM] * 4 + [VMEM] * 2, limit=LARGE, out_specs=[VMEM] * 2, scratch_shapes=[pltpu.VMEM((BS, 128), F32)])
    rows = lax.all_to_all(own, "z", 0, 0)
    pieces = [rows] + [lax.ppermute(rows, HL, [(i, (i + k) % NY) for i in range(NY)]) for k in range(1, NY)]
    asked = [wants] + [shift(wants, k) for k in range(1, NX)]
    swapped = prep(tiles)
    *others, swapped, asked = lax.optimization_barrier((*pieces[1:], swapped, asked))
    pieces = pieces[:1] + others
    pieces += [lax.ppermute(p, "c", [(0, 1), (1, 0)]) for p in pieces]
    y = lax.axis_index(HL).reshape(1)
    picked = call(pick_kernel, "pick", [((2, 2, 4, 16, 128), BF16)] * NX, lax.axis_index("c").reshape(1), y, *asked, *pieces,
                  spaces=[SMEM] * 2 + [VMEM] * (NX + 2 * NY), out_specs=[VMEM] * NX,
                  scratch_shapes=[pltpu.VMEM((2, NY, 8, BS, 128), BF16)])
    got = [picked[0]] + [shift(picked[NX - k], k) for k in range(1, NX)]
    pieces = tile_pairs(me, tiles, swapped, wants, got)
    terms = lax.all_to_all(pieces, CX, 0, 0)
    dense = call(place_kernel, "place", ((32, 16, 128), BF16), terms, out_specs=VMEM)
    spread = lax.all_to_all(dense, ZHL, 0, 0)
    owned = call(sum_kernel, "sum", ((NG, 8, 128), F32), spread, out_specs=VMEM)
    parts = lax.all_to_all(owned, CX, 0, 0)
    out = call(finish_kernel, "finish", ((BS, AUX * BS), F32), parts,
               out_specs=pl.BlockSpec((BS, AUX * BS), lambda: (0, 0)),
               scratch_shapes=[pltpu.VMEM((AUX, 32, 128), F32)])
    return out.T


def solution(mesh):
    fine = Mesh(mesh.devices.reshape(8, 2, 2, 2, 4), ALL)
    return jax.shard_map(
        shards,
        mesh=fine,
        in_specs=(P(ALL, None, None), P(ALL), P(ALL), P(ALL), P(ALL), P(ALL, None), P(ALL, None)),
        out_specs=P(TENS, None),
        check_vma=False,
    )
```

```python
import jax
import jax.numpy as jnp
from jax import lax
from jax.experimental import pallas as pl
from jax.experimental.pallas import tpu as pltpu
from jax.sharding import Mesh, PartitionSpec as P

BS = 64
NA = 16
AUX = 2
ZHL = ("z", "h", "l")
HL = ("h", "l")
CX = ("c", "x")
TENS = ("z", "h", "l", "c")
ALL = ("z", "h", "l", "c", "x")
NX = NY = 4
NG = 8
F32, BF16 = jnp.float32, jnp.bfloat16
VMEM = pl.BlockSpec(memory_space=pltpu.VMEM)
SMEM = pl.BlockSpec(memory_space=pltpu.SMEM)
LARGE, MIDDLE, SMALL = 58 * 1024 * 1024, 52 * 1024 * 1024, 12 * 1024 * 1024
PITCH = 65


def shift(values, k):
    return lax.ppermute(values, "x", [(i, (i + k) % NX) for i in range(NX)])


def low_lanes(rows):
    return lax.broadcasted_iota(jnp.int32, (rows, 128), 1) < BS


def rows_kernel(row_ref, col_ref, dest_ref, aux_ref, occ_ref, virt_ref, o_ref, wants_ref, scr):
    at = lax.broadcasted_iota(jnp.int32, (8, 128), 0)
    for j in range(3):
        found = jnp.zeros((8, 128), jnp.int32)
        for t in range(8):
            value = row_ref[t] if j == 0 else col_ref[t] if j == 1 else dest_ref[t] * AUX + aux_ref[t]
            found = jnp.where(at == t, value, found)
        wants_ref[j] = found
    for arr, ref in enumerate((occ_ref, virt_ref)):
        values = ref[...].astype(F32)
        for i in range(4):
            for pair in range(8):
                at = (arr * 4 + i) * 8 + pair
                scr[at:at + 1, :] = values[i:i + 1, pair * 128:pair * 128 + 128]
    block = scr[...].astype(BF16)
    for peer in range(o_ref.shape[0]):
        o_ref[peer] = block


def prep_kernel(t_ref, sw_ref, scr):
    for s in range(16):
        cut = slice(s * 256, s * 256 + 256)
        turned = jnp.concatenate([t_ref[0, :, cut], t_ref[1, :, cut]], axis=0).T
        for k in range(4):
            at = (4 * s + k) * PITCH
            scr[at:at + BS, :] = turned[k * BS:k * BS + BS].astype(F32)
    for s in range(16):
        cut = slice(s * 256, s * 256 + 256)
        rows = jnp.concatenate([scr[pl.ds(4 * s + k, BS, stride=PITCH), :] for k in range(4)], axis=0)
        back = rows.astype(BF16).T
        sw_ref[0, :, cut] = back[:BS]
        sw_ref[1, :, cut] = back[BS:]


def prep(tiles):
    count = tiles.shape[0]
    spec = pl.BlockSpec((2, BS, BS * BS), lambda i: (i, 0, 0))
    return pl.pallas_call(
        prep_kernel,
        grid=(count // 2,),
        out_shape=jax.ShapeDtypeStruct(tiles.shape, BF16),
        in_specs=[spec],
        out_specs=spec,
        scratch_shapes=[pltpu.VMEM((BS * PITCH, 128), F32)],
        cost_estimate=pl.CostEstimate(flops=9_000_000_000, bytes_accessed=4 * tiles.size, transcendentals=0),
        compiler_params=pltpu.CompilerParams(vmem_limit_bytes=LARGE),
        name="prep",
    )(tiles)


def pick_kernel(core_ref, y_ref, w0, w1, w2, w3, *refs):
    pieces, (o0, o1, o2, o3, rows) = refs[:2 * NY], refs[2 * NY:]
    for k in range(NY):
        y = (y_ref[0] - k + NY) & 3
        rows[core_ref[0], y] = pieces[k][...]
        rows[1 - core_ref[0], y] = pieces[NY + k][...]
    row, col = (jnp.concatenate([w[j] for w in (w0, w1, w2, w3)], axis=0) for j in range(2))
    lane = lax.broadcasted_iota(jnp.int32, (32, 128), 1)
    low = low_lanes(32)
    hots = []
    for arr, first in enumerate((row, col)):
        hot = []
        for q in range(2):
            second = first if q == 0 else (col if arr == 0 else row)
            for odd in range(2):
                for i in range(2):
                    key = jnp.where((second & 1) == odd, first * 16 + i * 8 + (second >> 1), -1)
                    hot.append(jnp.concatenate([
                        jnp.where(lane == key, 1.0, 0.0).astype(BF16),
                        jnp.where(lane + 128 == key, 1.0, 0.0).astype(BF16),
                    ], axis=1))
        hots.append(jnp.concatenate(hot, axis=0))
    for side in range(2):
        for l in range(2):
            for ih in range(2):
                got = []
                for arr in range(2):
                    start = (arr * 2 + ih) * 16
                    table = jnp.concatenate([rows[side, 2 * (b % 2) + l, b // 2, start:start + 16, :] for b in range(NA)], axis=0)
                    got.append(jnp.dot(hots[arr], table, preferred_element_type=F32))
                for il in range(2):
                    found = []
                    for arr in range(2):
                        g = [got[arr][(k * 2 + il) * 32:(k * 2 + il) * 32 + 32] for k in range(4)]
                        left = g[0] + pltpu.roll(g[1], BS, 1)
                        right = pltpu.roll(g[2], BS, 1) + g[3]
                        found.append(jnp.where(low, left, right))
                    for k, o_ref in enumerate((o0, o1, o2, o3)):
                        cut = slice(k * 8, k * 8 + 8)
                        o_ref[l, side, ih * 2 + il] = jnp.concatenate([f[cut] for f in found], axis=0).astype(BF16)


def tile_kernel(me_ref, t_ref, sw_ref, wants_ref, g0, g1, g2, g3, o_ref, gscr, us, ws, ys, zs, pk):
    step = pl.program_id(0)

    @pl.when(step == 0)
    def _():
        for k, ref in enumerate((g0, g1, g2, g3)):
            first = ((me_ref[0] - k + NX) & 3) * 4
            for l in range(2):
                for c in range(2):
                    for i in range(4):
                        at = pl.multiple_of((first + (l * 32 + c * 16 + i)) * 24, 8)
                        gscr[pl.ds(at, 16), :] = ref[l, c, i].astype(F32)

    low = low_lanes(BS)

    def blocks_t(arr, u):
        rows = gscr[pl.ds(arr * 8 + step * 2 + u, BS, stride=24), :]
        turned = jnp.concatenate([rows, rows], axis=0).T
        return turned[:BS], turned[BS:]

    def two(b):
        return jnp.concatenate([jnp.where(low, b, 0.0), jnp.where(low, 0.0, b)], axis=0).astype(BF16)

    def four(b):
        pair = two(b)
        none = jnp.zeros((128, 128), BF16)
        return jnp.concatenate([jnp.concatenate([pair, none], axis=1), jnp.concatenate([none, pair], axis=1)], axis=0)

    (cc0, cr0), (cc1, cr1) = blocks_t(1, 0), blocks_t(1, 1)
    virt = jnp.concatenate([
        jnp.concatenate([two(cc0), two(cc1)], axis=1),
        jnp.concatenate([two(cr0), two(cr1)], axis=1),
    ], axis=0)
    low128 = low_lanes(128)
    zero = jnp.zeros((128, 128), BF16)
    for s in range(16):
        cut = slice(s * 256, s * 256 + 256)
        turned = jnp.concatenate([t_ref[0, :, cut], t_ref[1, :, cut]], axis=0).T
        a, b = turned[:128], turned[128:]
        rhs = jnp.concatenate([
            jnp.concatenate([jnp.where(low128, a, zero), jnp.where(low128, b, zero)], axis=1),
            jnp.concatenate([jnp.where(low128, zero, a), jnp.where(low128, zero, b)], axis=1),
        ], axis=0)
        out = jnp.dot(virt, rhs, preferred_element_type=F32)
        for ref, first in ((us, 0), (ws, 128)):
            for k in range(4):
                at, row, lane = (4 * s + k) * PITCH, first + (k % 2) * BS, (k // 2) * 128
                ref[at:at + BS, :] = out[row:row + BS, lane:lane + 128]
    for u in range(2):
        same, cross = blocks_t(0, u)
        for ref, dest, block in ((sw_ref, ys, same), (t_ref, zs, cross)):
            rows = jnp.concatenate([ref[u, :, s * 256:s * 256 + 256] for s in range(16)], axis=0)
            out = jnp.dot(rows, four(block), preferred_element_type=F32).astype(BF16)
            for s in range(16):
                dest[u * BS:u * BS + BS, s * 256:s * 256 + 256] = out[s * BS:s * BS + BS]
    acc = jnp.zeros((128, 128), F32)
    for left, right in ((ys, us), (zs, ws)):
        for s in range(16):
            rows = jnp.concatenate([right[pl.ds(4 * s + k, BS, stride=PITCH), :] for k in range(4)], axis=0)
            acc += jnp.dot(left[:, s * 256:s * 256 + 256], rows.astype(BF16), preferred_element_type=F32)
    acc = acc * (1.0 / BS)
    low32 = low_lanes(32)
    packed = (
        jnp.where(low32, acc[:32], pltpu.roll(acc[32:64], BS, 1)),
        jnp.where(low32, pltpu.roll(acc[64:96], BS, 1), acc[96:]),
    )
    for u in range(2):
        pk[pl.ds(pl.multiple_of((step * 2 + u) * 40, 8), 32), :] = packed[u]

    @pl.when(step == pl.num_programs(0) - 1)
    def _():
        target = wants_ref[2].astype(F32)
        target = jnp.concatenate([target, target], axis=0).astype(BF16)
        for peer in range(NG):
            for r in (0, 2):
                rows = [pk[pl.ds(4 * peer + r + i, 8, stride=40), :] for i in range(2)]
                o_ref[peer, r * 8:r * 8 + 16] = jnp.concatenate(rows, axis=0).astype(BF16)
            o_ref[peer, 32:48] = target


def tile_pairs(me, tiles, swapped, wants, got):
    count = tiles.shape[0]
    tile = pl.BlockSpec((2, BS, BS * BS), lambda i: (i, 0, 0))
    return pl.pallas_call(
        tile_kernel,
        grid=(count // 2,),
        out_shape=jax.ShapeDtypeStruct((NG, 6 * count, 128), BF16),
        in_specs=[SMEM, tile, tile] + [VMEM] * 5,
        out_specs=pl.BlockSpec((NG, 6 * count, 128), lambda i: (0, 0, 0)),
        scratch_shapes=[
            pltpu.VMEM((BS * 24, 128), F32), pltpu.VMEM((BS * PITCH, 128), F32), pltpu.VMEM((BS * PITCH, 128), F32),
            pltpu.VMEM((128, BS * BS), BF16), pltpu.VMEM((128, BS * BS), BF16), pltpu.VMEM((count * 40, 128), F32),
        ],
        compiler_params=pltpu.CompilerParams(vmem_limit_bytes=MIDDLE),
        name="tile_pairs",
    )(me, tiles, swapped, wants, *got)


def place_kernel(t_ref, o_ref):
    given = t_ref[...].astype(F32)
    target = given[:, 32:40, :].reshape(64, 128)
    target = jnp.concatenate([target, target], axis=0).T.astype(jnp.int32)
    lane = lax.broadcasted_iota(jnp.int32, (128, 128), 1)
    terms = jnp.concatenate([given[:, r * 8:r * 8 + 8, :].reshape(64, 128) for r in range(4)], axis=0).astype(BF16)
    for part in range(4):
        row = lax.broadcasted_iota(jnp.int32, (128, 128), 0) + part * 128
        here = ((row >> 4) == (target >> 2)) & ((row & 3) == (target & 3))
        hot = jnp.concatenate([
            jnp.where(here & (((row >> 2) & 3) == (lane >> 6) + 2 * half), 1.0, 0.0).astype(BF16) for half in range(2)
        ], axis=1)
        dense = jnp.dot(hot, terms, preferred_element_type=F32)
        o_ref[part * 8:part * 8 + 8] = dense.astype(BF16).reshape(8, 16, 128)


def sum_kernel(s_ref, o_ref):
    total = jnp.sum(s_ref[...].astype(F32), axis=0)
    for core in range(2):
        at = [r * 4 + core * 2 + aux for aux in range(AUX) for r in range(4)]
        rows = jnp.concatenate([total[i:i + 1] for i in at], axis=0)
        for x in range(NX):
            o_ref[core * NX + x] = rows


def finish_kernel(p_ref, o_ref, whole):
    for aux in range(AUX):
        for peer in range(NG):
            whole[aux, 4 * peer:4 * peer + 4, :] = p_ref[peer, 4 * aux:4 * aux + 4, :]
    one, two = whole[0], whole[1]
    low = low_lanes(32)
    o_ref[:32, :] = jnp.where(low, one, pltpu.roll(two, BS, 1))
    o_ref[32:, :] = jnp.where(low, pltpu.roll(one, BS, 1), two)


def call(kernel, name, out, *args, spaces=None, limit=SMALL, **more):
    return pl.pallas_call(
        kernel,
        out_shape=[jax.ShapeDtypeStruct(*s) for s in out] if isinstance(out, list) else jax.ShapeDtypeStruct(*out),
        in_specs=spaces or [VMEM] * len(args),
        compiler_params=pltpu.CompilerParams(vmem_limit_bytes=limit),
        name=name,
        **more,
    )(*args)


def shards(tiles, tile_dest, tile_aux, tile_row, tile_col, green_occ, green_virt):
    me = lax.axis_index("x").reshape(1)
    own, wants = call(rows_kernel, "rows", [((8, BS, 128), BF16), ((3, 8, 128), jnp.int32)],
                      tile_row, tile_col, tile_dest, tile_aux, green_occ, green_virt,
                      spaces=[SMEM] * 4 + [VMEM] * 2, limit=LARGE, out_specs=[VMEM] * 2, scratch_shapes=[pltpu.VMEM((BS, 128), F32)])
    rows = lax.all_to_all(own, "z", 0, 0)
    pieces = [rows] + [lax.ppermute(rows, HL, [(i, (i + k) % NY) for i in range(NY)]) for k in range(1, NY)]
    asked = [wants] + [shift(wants, k) for k in range(1, NX)]
    swapped = prep(tiles)
    *others, swapped, asked = lax.optimization_barrier((*pieces[1:], swapped, asked))
    pieces = pieces[:1] + others
    pieces += [lax.ppermute(p, "c", [(0, 1), (1, 0)]) for p in pieces]
    y = lax.axis_index(HL).reshape(1)
    picked = call(pick_kernel, "pick", [((2, 2, 4, 16, 128), BF16)] * NX, lax.axis_index("c").reshape(1), y, *asked, *pieces,
                  spaces=[SMEM] * 2 + [VMEM] * (NX + 2 * NY), out_specs=[VMEM] * NX,
                  scratch_shapes=[pltpu.VMEM((2, NY, 8, BS, 128), BF16)])
    got = [picked[0]] + [shift(picked[NX - k], k) for k in range(1, NX)]
    pieces = tile_pairs(me, tiles, swapped, wants, got)
    terms = lax.all_to_all(pieces, CX, 0, 0)
    dense = call(place_kernel, "place", ((32, 16, 128), BF16), terms, out_specs=VMEM)
    spread = lax.all_to_all(dense, ZHL, 0, 0)
    owned = call(sum_kernel, "sum", ((NG, 8, 128), F32), spread, out_specs=VMEM)
    parts = lax.all_to_all(owned, CX, 0, 0)
    out = call(finish_kernel, "finish", ((BS, AUX * BS), F32), parts,
               out_specs=pl.BlockSpec((BS, AUX * BS), lambda: (0, 0)),
               scratch_shapes=[pltpu.VMEM((AUX, 32, 128), F32)])
    return out.T


def solution(mesh):
    fine = Mesh(mesh.devices.reshape(8, 2, 2, 2, 4), ALL)
    return jax.shard_map(
        shards,
        mesh=fine,
        in_specs=(P(ALL, None, None), P(ALL), P(ALL), P(ALL), P(ALL), P(ALL, None), P(ALL, None)),
        out_specs=P(TENS, None),
        check_vma=False,
    )
```

```python
import jax
import jax.numpy as jnp
from jax import lax
from jax.experimental import pallas as pl
from jax.experimental.pallas import tpu as pltpu
from jax.sharding import Mesh, PartitionSpec as P

BS = 64
NA = 16
AUX = 2
ZHL = ("z", "h", "l")
HL = ("h", "l")
CX = ("c", "x")
TENS = ("z", "h", "l", "c")
ALL = ("z", "h", "l", "c", "x")
NX = NY = 4
NG = 8
F32, BF16 = jnp.float32, jnp.bfloat16
VMEM = pl.BlockSpec(memory_space=pltpu.VMEM)
SMEM = pl.BlockSpec(memory_space=pltpu.SMEM)
LARGE, MIDDLE, SMALL = 58 * 1024 * 1024, 52 * 1024 * 1024, 12 * 1024 * 1024
PITCH = 65


def shift(values, k):
    return lax.ppermute(values, "x", [(i, (i + k) % NX) for i in range(NX)])


def low_lanes(rows):
    return lax.broadcasted_iota(jnp.int32, (rows, 128), 1) < BS


def rows_kernel(row_ref, col_ref, dest_ref, aux_ref, occ_ref, virt_ref, o_ref, wants_ref, target_ref, scr):
    at = lax.broadcasted_iota(jnp.int32, (8, 128), 0)
    for j in range(3):
        found = jnp.zeros((8, 128), jnp.int32)
        for t in range(8):
            value = row_ref[t] if j == 0 else col_ref[t] if j == 1 else dest_ref[t] * AUX + aux_ref[t]
            found = jnp.where(at == t, value, found)
        if j < 2:
            wants_ref[j] = found
        else:
            target_ref[...] = jnp.concatenate([found, found], axis=0).astype(F32).astype(BF16)
    for arr, ref in enumerate((occ_ref, virt_ref)):
        values = ref[...].astype(F32)
        for i in range(4):
            for pair in range(8):
                at = (arr * 4 + i) * 8 + pair
                scr[at:at + 1, :] = values[i:i + 1, pair * 128:pair * 128 + 128]
    block = scr[...].astype(BF16)
    for peer in range(o_ref.shape[0]):
        o_ref[peer] = block


def prep_kernel(t_ref, sw_ref, scr):
    for s in range(16):
        cut = slice(s * 256, s * 256 + 256)
        turned = jnp.concatenate([t_ref[0, :, cut], t_ref[1, :, cut]], axis=0).T
        for k in range(4):
            at = (4 * s + k) * PITCH
            scr[at:at + BS, :] = turned[k * BS:k * BS + BS].astype(F32)
    for s in range(16):
        cut = slice(s * 256, s * 256 + 256)
        rows = jnp.concatenate([scr[pl.ds(4 * s + k, BS, stride=PITCH), :] for k in range(4)], axis=0)
        back = rows.astype(BF16).T
        sw_ref[0, :, cut] = back[:BS]
        sw_ref[1, :, cut] = back[BS:]


def prep(tiles):
    count = tiles.shape[0]
    spec = pl.BlockSpec((2, BS, BS * BS), lambda i: (i, 0, 0))
    return pl.pallas_call(
        prep_kernel,
        grid=(count // 2,),
        out_shape=jax.ShapeDtypeStruct(tiles.shape, BF16),
        in_specs=[spec],
        out_specs=spec,
        scratch_shapes=[pltpu.VMEM((BS * PITCH, 128), F32)],
        cost_estimate=pl.CostEstimate(flops=9_000_000_000, bytes_accessed=4 * tiles.size, transcendentals=0),
        compiler_params=pltpu.CompilerParams(vmem_limit_bytes=LARGE),
        name="prep",
    )(tiles)


def pick_kernel(core_ref, y_ref, w0, w1, w2, w3, *refs):
    pieces, (o0, o1, o2, o3, rows) = refs[:2 * NY], refs[2 * NY:]
    for k in range(NY):
        y = (y_ref[0] - k + NY) & 3
        rows[core_ref[0], y] = pieces[k][...]
        rows[1 - core_ref[0], y] = pieces[NY + k][...]
    row, col = (jnp.concatenate([w[j] for w in (w0, w1, w2, w3)], axis=0) for j in range(2))
    lane = lax.broadcasted_iota(jnp.int32, (32, 128), 1)
    low = low_lanes(32)
    hots = []
    for arr, first in enumerate((row, col)):
        hot = []
        for q in range(2):
            second = first if q == 0 else (col if arr == 0 else row)
            for odd in range(2):
                for i in range(2):
                    key = jnp.where((second & 1) == odd, first * 16 + i * 8 + (second >> 1), -1)
                    hot.append(jnp.concatenate([
                        jnp.where(lane == key, 1.0, 0.0).astype(BF16),
                        jnp.where(lane + 128 == key, 1.0, 0.0).astype(BF16),
                    ], axis=1))
        hots.append(jnp.concatenate(hot, axis=0))
    for side in range(2):
        for l in range(2):
            for ih in range(2):
                got = []
                for arr in range(2):
                    start = (arr * 2 + ih) * 16
                    table = jnp.concatenate([rows[side, 2 * (b % 2) + l, b // 2, start:start + 16, :] for b in range(NA)], axis=0)
                    got.append(jnp.dot(hots[arr], table, preferred_element_type=F32))
                for il in range(2):
                    found = []
                    for arr in range(2):
                        g = [got[arr][(k * 2 + il) * 32:(k * 2 + il) * 32 + 32] for k in range(4)]
                        left = g[0] + pltpu.roll(g[1], BS, 1)
                        right = pltpu.roll(g[2], BS, 1) + g[3]
                        found.append(jnp.where(low, left, right))
                    for k, o_ref in enumerate((o0, o1, o2, o3)):
                        cut = slice(k * 8, k * 8 + 8)
                        o_ref[l, side, ih * 2 + il] = jnp.concatenate([f[cut] for f in found], axis=0).astype(BF16)


def tile_kernel(me_ref, t_ref, sw_ref, target_ref, g0, g1, g2, g3, o_ref, gscr, us, ws, ys, zs, pk):
    step = pl.program_id(0)

    @pl.when(step == 0)
    def _():
        for k, ref in enumerate((g0, g1, g2, g3)):
            first = ((me_ref[0] - k + NX) & 3) * 4
            for l in range(2):
                for c in range(2):
                    for i in range(4):
                        at = pl.multiple_of((first + (l * 32 + c * 16 + i)) * 24, 8)
                        gscr[pl.ds(at, 16), :] = ref[l, c, i].astype(F32)

    low = low_lanes(BS)

    def blocks_t(arr, u):
        rows = gscr[pl.ds(arr * 8 + step * 2 + u, BS, stride=24), :]
        turned = jnp.concatenate([rows, rows], axis=0).T
        return turned[:BS], turned[BS:]

    def two(b):
        return jnp.concatenate([jnp.where(low, b, 0.0), jnp.where(low, 0.0, b)], axis=0).astype(BF16)

    def four(b):
        pair = two(b)
        none = jnp.zeros((128, 128), BF16)
        return jnp.concatenate([jnp.concatenate([pair, none], axis=1), jnp.concatenate([none, pair], axis=1)], axis=0)

    (cc0, cr0), (cc1, cr1) = blocks_t(1, 0), blocks_t(1, 1)
    virt = jnp.concatenate([
        jnp.concatenate([two(cc0), two(cc1)], axis=1),
        jnp.concatenate([two(cr0), two(cr1)], axis=1),
    ], axis=0)
    low128 = low_lanes(128)
    zero = jnp.zeros((128, 128), BF16)
    for s in range(16):
        cut = slice(s * 256, s * 256 + 256)
        turned = jnp.concatenate([t_ref[0, :, cut], t_ref[1, :, cut]], axis=0).T
        a, b = turned[:128], turned[128:]
        rhs = jnp.concatenate([
            jnp.concatenate([jnp.where(low128, a, zero), jnp.where(low128, b, zero)], axis=1),
            jnp.concatenate([jnp.where(low128, zero, a), jnp.where(low128, zero, b)], axis=1),
        ], axis=0)
        out = jnp.dot(virt, rhs, preferred_element_type=F32)
        for ref, first in ((us, 0), (ws, 128)):
            for k in range(4):
                at, row, lane = (4 * s + k) * PITCH, first + (k % 2) * BS, (k // 2) * 128
                ref[at:at + BS, :] = out[row:row + BS, lane:lane + 128]
    for u in range(2):
        same, cross = blocks_t(0, u)
        for ref, dest, block in ((sw_ref, ys, same), (t_ref, zs, cross)):
            rows = jnp.concatenate([ref[u, :, s * 256:s * 256 + 256] for s in range(16)], axis=0)
            out = jnp.dot(rows, four(block), preferred_element_type=F32).astype(BF16)
            for s in range(16):
                dest[u * BS:u * BS + BS, s * 256:s * 256 + 256] = out[s * BS:s * BS + BS]
    acc = jnp.zeros((128, 128), F32)
    for left, right in ((ys, us), (zs, ws)):
        for s in range(16):
            rows = jnp.concatenate([right[pl.ds(4 * s + k, BS, stride=PITCH), :] for k in range(4)], axis=0)
            acc += jnp.dot(left[:, s * 256:s * 256 + 256], rows.astype(BF16), preferred_element_type=F32)
    acc = acc * (1.0 / BS)
    low32 = low_lanes(32)
    packed = (
        jnp.where(low32, acc[:32], pltpu.roll(acc[32:64], BS, 1)),
        jnp.where(low32, pltpu.roll(acc[64:96], BS, 1), acc[96:]),
    )
    for u in range(2):
        pk[pl.ds(pl.multiple_of((step * 2 + u) * 40, 8), 32), :] = packed[u]

    @pl.when(step == pl.num_programs(0) - 1)
    def _():
        target = target_ref[...]
        for peer in range(NG):
            for r in (0, 2):
                rows = [pk[pl.ds(4 * peer + r + i, 8, stride=40), :] for i in range(2)]
                o_ref[peer, r * 8:r * 8 + 16] = jnp.concatenate(rows, axis=0).astype(BF16)
            o_ref[peer, 32:48] = target


def tile_pairs(me, tiles, swapped, target, got):
    count = tiles.shape[0]
    tile = pl.BlockSpec((2, BS, BS * BS), lambda i: (i, 0, 0))
    return pl.pallas_call(
        tile_kernel,
        grid=(count // 2,),
        out_shape=jax.ShapeDtypeStruct((NG, 6 * count, 128), BF16),
        in_specs=[SMEM, tile, tile] + [VMEM] * 5,
        out_specs=pl.BlockSpec((NG, 6 * count, 128), lambda i: (0, 0, 0)),
        scratch_shapes=[
            pltpu.VMEM((BS * 24, 128), F32), pltpu.VMEM((BS * PITCH, 128), F32), pltpu.VMEM((BS * PITCH, 128), F32),
            pltpu.VMEM((128, BS * BS), BF16), pltpu.VMEM((128, BS * BS), BF16), pltpu.VMEM((count * 40, 128), F32),
        ],
        compiler_params=pltpu.CompilerParams(vmem_limit_bytes=MIDDLE),
        name="tile_pairs",
    )(me, tiles, swapped, target, *got)


def place_kernel(t_ref, o_ref):
    given = t_ref[...].astype(F32)
    target = given[:, 32:40, :].reshape(64, 128)
    target = jnp.concatenate([target, target], axis=0).T.astype(jnp.int32)
    lane = lax.broadcasted_iota(jnp.int32, (128, 128), 1)
    terms = jnp.concatenate([given[:, r * 8:r * 8 + 8, :].reshape(64, 128) for r in range(4)], axis=0).astype(BF16)
    for part in range(4):
        row = lax.broadcasted_iota(jnp.int32, (128, 128), 0) + part * 128
        here = ((row >> 4) == (target >> 2)) & ((row & 3) == (target & 3))
        hot = jnp.concatenate([
            jnp.where(here & (((row >> 2) & 3) == (lane >> 6) + 2 * half), 1.0, 0.0).astype(BF16) for half in range(2)
        ], axis=1)
        dense = jnp.dot(hot, terms, preferred_element_type=F32)
        o_ref[part * 8:part * 8 + 8] = dense.astype(BF16).reshape(8, 16, 128)


def sum_kernel(s_ref, o_ref):
    total = jnp.sum(s_ref[...].astype(F32), axis=0)
    for core in range(2):
        at = [r * 4 + core * 2 + aux for aux in range(AUX) for r in range(4)]
        rows = jnp.concatenate([total[i:i + 1] for i in at], axis=0)
        for x in range(NX):
            o_ref[core * NX + x] = rows


def finish_kernel(p_ref, o_ref, whole):
    for aux in range(AUX):
        for peer in range(NG):
            whole[aux, 4 * peer:4 * peer + 4, :] = p_ref[peer, 4 * aux:4 * aux + 4, :]
    one, two = whole[0], whole[1]
    low = low_lanes(32)
    o_ref[:32, :] = jnp.where(low, one, pltpu.roll(two, BS, 1))
    o_ref[32:, :] = jnp.where(low, pltpu.roll(one, BS, 1), two)


def call(kernel, name, out, *args, spaces=None, limit=SMALL, **more):
    return pl.pallas_call(
        kernel,
        out_shape=[jax.ShapeDtypeStruct(*s) for s in out] if isinstance(out, list) else jax.ShapeDtypeStruct(*out),
        in_specs=spaces or [VMEM] * len(args),
        compiler_params=pltpu.CompilerParams(vmem_limit_bytes=limit),
        name=name,
        **more,
    )(*args)


def shards(tiles, tile_dest, tile_aux, tile_row, tile_col, green_occ, green_virt):
    me = lax.axis_index("x").reshape(1)
    own, wants, target = call(rows_kernel, "rows", [((8, BS, 128), BF16), ((2, 8, 128), jnp.int32), ((16, 128), BF16)],
                      tile_row, tile_col, tile_dest, tile_aux, green_occ, green_virt,
                      spaces=[SMEM] * 4 + [VMEM] * 2, limit=LARGE, out_specs=[VMEM] * 3, scratch_shapes=[pltpu.VMEM((BS, 128), F32)])
    rows = lax.all_to_all(own, "z", 0, 0)
    pieces = [rows] + [lax.ppermute(rows, HL, [(i, (i + k) % NY) for i in range(NY)]) for k in range(1, NY)]
    asked = [wants] + [shift(wants, k) for k in range(1, NX)]
    swapped = prep(tiles)
    *others, swapped, asked = lax.optimization_barrier((*pieces[1:], swapped, asked))
    pieces = pieces[:1] + others
    pieces += [lax.ppermute(p, "c", [(0, 1), (1, 0)]) for p in pieces]
    y = lax.axis_index(HL).reshape(1)
    picked = call(pick_kernel, "pick", [((2, 2, 4, 16, 128), BF16)] * NX, lax.axis_index("c").reshape(1), y, *asked, *pieces,
                  spaces=[SMEM] * 2 + [VMEM] * (NX + 2 * NY), out_specs=[VMEM] * NX,
                  scratch_shapes=[pltpu.VMEM((2, NY, 8, BS, 128), BF16)])
    got = [picked[0]] + [shift(picked[NX - k], k) for k in range(1, NX)]
    pieces = tile_pairs(me, tiles, swapped, target, got)
    terms = lax.all_to_all(pieces, CX, 0, 0)
    dense = call(place_kernel, "place", ((32, 16, 128), BF16), terms, out_specs=VMEM)
    spread = lax.all_to_all(dense, ZHL, 0, 0)
    owned = call(sum_kernel, "sum", ((NG, 8, 128), F32), spread, out_specs=VMEM)
    parts = lax.all_to_all(owned, CX, 0, 0)
    out = call(finish_kernel, "finish", ((BS, AUX * BS), F32), parts,
               out_specs=pl.BlockSpec((BS, AUX * BS), lambda: (0, 0)),
               scratch_shapes=[pltpu.VMEM((AUX, 32, 128), F32)])
    return out.T


def solution(mesh):
    fine = Mesh(mesh.devices.reshape(8, 2, 2, 2, 4), ALL)
    return jax.shard_map(
        shards,
        mesh=fine,
        in_specs=(P(ALL, None, None), P(ALL), P(ALL), P(ALL), P(ALL), P(ALL, None), P(ALL, None)),
        out_specs=P(TENS, None),
        check_vma=False,
    )
```
